128 devices in a mesh: occ: 8 (over z_lo, x), emp: 16 (over z_hi, y, core).
Axes of the slice: x: 4, y: 4, z: 4 (z_hi: 2, z_lo: 2; z = z_hi * 2 + z_lo), core: 2. Of those that a mesh axis runs over, the one named last changes fastest.
Arguments:
- occupied: bfloat16 [2, 32, 96, 9216], P(None, 'occ', 'emp'), may hold values from -5 to 5
- empty: bfloat16 [2, 64, 96, 9216], P(None, 'emp', 'occ'), may hold values from -5 to 5
- occ_energy: float32 [32], P('occ'), may hold values from -0.8 to -0.1
- emp_energy: float32 [64], P('emp'), may hold values from 0.05 to 2
- gvec: int32 [8000], replicated, may hold values from 0 to 15624, as said below
Outputs:
- chi_zero: float32 [2, 8000, 8000], P(None, 'occ', 'emp')
The draws below stay inside these ranges and needn't reach their ends.
Inputs may be any that keep to these rules, and one draw needn't show every extreme that they name: gvec holds 8000 distinct box indices, those of the 8000 frequencies of smallest length in the box (ties of equal length chosen at random), in a random order.
All inputs are finite; a program needn't handle non-finite values.
Results may differ from the reference program's by a relative error of at most 0.0038.
Values may be sent and summed in bfloat16 or wider, within the bound.
A program may use at most 192 MiB of HBM per device.

```python
import math
import jax
import jax.numpy as jnp
from jax import lax

GRID = 96
KB = 25
NG = 8000
NV = 32
NC = 64


def draw_gvec(key, part):
    key = jax.random.fold_in(key, 7)
    first_key, second_key = jax.random.split(key)
    freq_index = (jnp.arange(KB, dtype=jnp.int32) + KB // 2) % KB - KB // 2
    lengths = (freq_index[:, None, None] ** 2 + freq_index[None, :, None] ** 2 + freq_index[None, None, :] ** 2).reshape(-1)
    tiebreak = jax.random.permutation(first_key, KB ** 3).astype(jnp.int32)
    scores = -(lengths * KB ** 3 + tiebreak)
    unused, chosen = lax.top_k(scores, NG)
    shuffle = jax.random.permutation(second_key, NG)
    return chosen[shuffle].astype(jnp.int32)


def block_levels(rng, shape, cuts, smallest, largest):
    def one(axis_at, shards_of):
        heights = jax.random.uniform(jax.random.fold_in(jax.random.fold_in(rng, 6), axis_at), (shards_of,), jnp.float32, smallest / len(cuts), largest / len(cuts))
        return jnp.repeat(jnp.exp(heights), shape[axis_at] // shards_of).reshape((-1,) + (1,) * (len(shape) - axis_at - 1))

    gain = one(*cuts[0])
    for cut in cuts[1:]:
        gain = gain * one(*cut)
    return gain


def gaussian(stream_key, extent, width, reach, cuts=(), held_as=jnp.bfloat16):
    loudness = block_levels(stream_key, extent, cuts, -0.22, 0.18) if cuts else 1.0
    entries = jax.random.normal(stream_key, extent, jnp.float32) * width * loudness
    return jnp.minimum(jnp.maximum(entries, -reach), reach).astype(held_as)


def setup_inputs(seed: int = 0) -> dict:
    key_of = jax.random.split(jax.random.key(seed), 6)
    occupied = gaussian(key_of[0], (2, NV, GRID, GRID * GRID), 0.7, 5.0, ((1, 8), (2, 16)))
    empty = gaussian(key_of[1], (2, NC, GRID, GRID * GRID), 0.7, 5.0, ((1, 16), (2, 8)))
    occ_energy = jnp.clip(-0.8 + 0.7 * jax.random.uniform(key_of[2], (NV,), jnp.float32) ** block_levels(key_of[2], (NV,), ((0, 8),), -0.2, 0.2), -0.8, -0.1)
    emp_energy = jnp.clip(0.05 + 1.95 * jax.random.uniform(key_of[3], (NC,), jnp.float32) ** block_levels(key_of[3], (NC,), ((0, 16),), -0.2, 0.2), 0.05, 2.0)
    gvec = draw_gvec(jax.random.fold_in(key_of[5], 71), 0)
    return {"occupied": occupied, "empty": empty, "occ_energy": occ_energy, "emp_energy": emp_energy, "gvec": gvec}


def reference(occupied, empty, occ_energy, emp_energy, gvec):
    signed_freq = (jnp.arange(KB) + KB // 2) % KB - KB // 2
    box_index = (signed_freq % GRID).astype(jnp.int32)
    emp_real = empty[0].astype(jnp.float32).reshape(NC, GRID, GRID, GRID)
    emp_imag = empty[1].astype(jnp.float32).reshape(NC, GRID, GRID, GRID)

    def densities_of(band):
        occ_real = occupied[0, band].astype(jnp.float32).reshape(1, GRID, GRID, GRID)
        occ_imag = occupied[1, band].astype(jnp.float32).reshape(1, GRID, GRID, GRID)
        prod_real = occ_real * emp_real + occ_imag * emp_imag
        prod_imag = occ_real * emp_imag - occ_imag * emp_real
        spectrum = jnp.fft.fftn(prod_real + 1j * prod_imag, axes=(1, 2, 3))
        box_values = spectrum[:, box_index][:, :, box_index][:, :, :, box_index].reshape(NC, KB ** 3)
        sphere = jnp.take(box_values, gvec, axis=1)
        weight = jnp.sqrt(4.0 / (emp_energy - occ_energy[band])) / math.sqrt(GRID ** 3)
        return jnp.stack([jnp.real(sphere) * weight[:, None], jnp.imag(sphere) * weight[:, None]]).astype(jnp.bfloat16)
    densities = lax.map(densities_of, jnp.arange(NV))
    stacked = densities.transpose(1, 0, 2, 3).reshape(2, NV * NC, NG).astype(jnp.float32)
    real_part = stacked[0]
    imag_part = stacked[1]
    highest = lax.Precision.HIGHEST
    real_out = jnp.dot(real_part.T, real_part, precision=highest, preferred_element_type=jnp.float32)
    real_out = real_out + jnp.dot(imag_part.T, imag_part, precision=highest, preferred_element_type=jnp.float32)
    imag_out = jnp.dot(imag_part.T, real_part, precision=highest, preferred_element_type=jnp.float32)
    imag_out = imag_out - jnp.dot(real_part.T, imag_part, precision=highest, preferred_element_type=jnp.float32)
    factor = -1.0 / math.sqrt(NV * NC)
    return jnp.stack([real_out * factor, imag_out * factor])
```

```python
import functools
import math

import jax
import jax.numpy as jnp
import ml_dtypes
import numpy as np
from jax import lax
from jax.experimental import pallas as pl
from jax.experimental.pallas import tpu as pltpu
from jax.sharding import PartitionSpec as P

GRID = 96
KB = 25
REACH = KB // 2
NG = 8000
RSQ = 153
GROUPS = 24
HALF = 256
KZ = 32
BLOCK = 500
BLOCK_PAD = 512

f32 = jnp.float32
bf16 = jnp.bfloat16


def split(table):
    high = table.astype(ml_dtypes.bfloat16)
    low = (table - high.astype(np.float64)).astype(ml_dtypes.bfloat16)
    return high, low


def half_disc():
    kept = []
    for kx in range(-REACH, REACH + 1):
        for ky in range(-REACH, REACH + 1):
            if kx * kx + ky * ky <= RSQ and (kx > 0 or (kx == 0 and ky >= 0)):
                kept.append((kx, ky))
    return np.array(kept)


def tables():
    theta = 2.0 * np.pi / GRID
    disc = half_disc()
    kx, ky = disc[:, 0], disc[:, 1]
    freq = (np.arange(KB) + REACH) % KB - REACH
    angle = theta * (np.outer(np.arange(GRID), freq) % GRID)
    first = np.zeros((2, 4, GRID, 2, 4, KZ))
    for y in range(4):
        first[0, y, :, 0, y, :KB] = np.cos(angle)
        first[0, y, :, 1, y, :KB] = -np.sin(angle)
        first[1, y, :, 0, y, :KB] = np.sin(angle)
        first[1, y, :, 1, y, :KB] = np.cos(angle)
    first = first.reshape(768, 256)
    j = np.repeat(np.arange(GROUPS), GRID)
    x = np.tile(np.arange(GRID), GROUPS)
    angle = theta * ((np.outer(kx, x) + 4 * np.outer(ky, j)) % GRID)
    second = np.zeros((2, HALF, GROUPS * GRID))
    second[0, : len(disc)] = np.cos(angle)
    second[1, : len(disc)] = np.sin(angle)
    second = second.reshape(2 * HALF, GROUPS * GRID)
    angle = theta * ((ky[:, None] * np.repeat(np.arange(4), KZ)[None, :]) % GRID)
    twiddle = np.zeros((2, HALF, 4 * KZ), np.float32)
    twiddle[0, : len(disc)] = np.cos(angle)
    twiddle[1, : len(disc)] = np.sin(angle)
    column = np.full((2, HALF), -1, np.int32)
    column[0, : len(disc)] = (kx % KB) * KB + ky % KB
    column[1, 1 : len(disc)] = ((-kx) % KB)[1:] * KB + ((-ky) % KB)[1:]
    return split(first), split(second), twiddle, column.reshape(2 * HALF, 1)


def pair_kernel(weight, occ, emp, t_hi, t_lo, a_hi, a_lo, tw, out, z_hi, z_lo):
    n_occ = occ.shape[1]
    c = pl.program_id(0)
    tile = 4

    def one_band(v, carry):
        def one_tile(jt, carry2):
            res = []
            ims = []
            for jj in range(tile):
                for q in range(3):
                    lanes = pl.ds(pl.multiple_of((jt * tile + jj) * 384 + q * 128, 128), 128)
                    vr = occ[0, v, :, lanes].astype(f32)
                    vi = occ[1, v, :, lanes].astype(f32)
                    cr = emp[0, 0, :, lanes].astype(f32)
                    ci = emp[1, 0, :, lanes].astype(f32)
                    res.append(vr * cr + vi * ci)
                    ims.append(vr * ci - vi * cr)
            rows = []
            rows_lo = []
            for jj in range(tile):
                parts = res[3 * jj : 3 * jj + 3] + ims[3 * jj : 3 * jj + 3]
                high = [p.astype(bf16) for p in parts]
                low = [(p - h.astype(f32)).astype(bf16) for p, h in zip(parts, high)]
                rows.append(jnp.concatenate(high, axis=1))
                rows_lo.append(jnp.concatenate(low, axis=1))
            high = jnp.concatenate(rows, axis=0)
            low = jnp.concatenate(rows_lo, axis=0)
            z = (
                jnp.dot(high, t_hi[...], preferred_element_type=f32)
                + jnp.dot(low, t_hi[...], preferred_element_type=f32)
                + jnp.dot(high, t_lo[...], preferred_element_type=f32)
            )
            zh = z.astype(bf16)
            where = pl.ds(pl.multiple_of(jt * (tile * GRID), 128), tile * GRID)
            z_hi[where, :] = zh
            z_lo[where, :] = (z - zh.astype(f32)).astype(bf16)
            return carry2

        lax.fori_loop(0, GROUPS // tile, one_tile, 0)
        both = (
            jnp.dot(a_hi[...], z_hi[...], preferred_element_type=f32)
            + jnp.dot(a_hi[...], z_lo[...], preferred_element_type=f32)
            + jnp.dot(a_lo[...], z_hi[...], preferred_element_type=f32)
        )
        ur = both[:HALF, :128]
        ui = both[:HALF, 128:]
        wr = both[HALF:, :128]
        wi = both[HALF:, 128:]
        cos, sin = tw[0], tw[1]
        w = weight[v, c]
        for sign in range(2):
            s = 1.0 - 2.0 * sign
            pr = ur + s * wi
            pi = ui - s * wr
            qr = (cos * pr + s * (sin * pi)).T
            qi = (cos * pi - s * (sin * pr)).T
            for at, q in ((0, qr), (1, qi)):
                total = (q[:KZ] + q[KZ : 2 * KZ]) + (q[2 * KZ : 3 * KZ] + q[3 * KZ :])
                out[at, v, 0, :, sign * HALF : (sign + 1) * HALF] = (total * w).astype(bf16)
        return carry

    lax.fori_loop(0, n_occ, one_band, 0)


def compact(weight, occ_all, emp_all):
    (t_hi, t_lo), (a_hi, a_lo), tw, unused = tables()
    n_occ, n_emp = occ_all.shape[1], emp_all.shape[1]
    whole = lambda shape: pl.BlockSpec(shape, lambda c: (0,) * len(shape), pipeline_mode=pl.Buffered(1))
    return pl.pallas_call(
        pair_kernel,
        grid=(n_emp,),
        out_shape=jax.ShapeDtypeStruct((2, n_occ, n_emp, KZ, 2 * HALF), bf16),
        in_specs=[
            pl.BlockSpec(memory_space=pltpu.SMEM),
            whole((2, n_occ, GRID, GRID * GRID)),
            pl.BlockSpec((2, 1, GRID, GRID * GRID), lambda c: (0, c, 0, 0)),
            whole((768, 256)),
            whole((768, 256)),
            whole((2 * HALF, GROUPS * GRID)),
            whole((2 * HALF, GROUPS * GRID)),
            whole((2, HALF, 128)),
        ],
        out_specs=pl.BlockSpec((2, n_occ, 1, KZ, 2 * HALF), lambda c: (0, 0, c, 0, 0)),
        scratch_shapes=[
            pltpu.VMEM((GROUPS * GRID, 256), bf16),
            pltpu.VMEM((GROUPS * GRID, 256), bf16),
        ],
        compiler_params=pltpu.CompilerParams(vmem_limit_bytes=58 * 2**20),
        name="pair_spectra",
    )(weight, occ_all, emp_all, t_hi, t_lo, a_hi, a_lo, tw)


def select_kernel(column, kxy, kz, x, out):
    hot = jnp.where(column[...] == kxy[0], 1.0, 0.0).astype(bf16)
    rows = x.shape[0] // KZ
    picked = jnp.dot(x[...], hot, preferred_element_type=f32)
    level = lax.broadcasted_iota(jnp.int32, (KZ, BLOCK_PAD), 0)
    mask = jnp.where(level == kz[0], 1.0, 0.0)
    total = jnp.sum(picked.reshape(rows, KZ, BLOCK_PAD) * mask[None], axis=1)
    out[0] = total.astype(bf16)


def select(gvec, x):
    column = tables()[3]
    blocks = NG // BLOCK
    padded = jnp.pad(gvec.reshape(blocks, 1, BLOCK), ((0, 0), (0, 0), (0, BLOCK_PAD - BLOCK)), constant_values=0)
    kxy = padded // KB
    kz = padded - kxy * KB
    live = lax.broadcasted_iota(jnp.int32, padded.shape, 2) < BLOCK
    kxy = jnp.where(live, kxy, -2)
    rows = x.shape[0] // KZ
    return pl.pallas_call(
        select_kernel,
        grid=(blocks,),
        out_shape=jax.ShapeDtypeStruct((blocks, rows, BLOCK_PAD), bf16),
        in_specs=[
            pl.BlockSpec((2 * HALF, 1), lambda b: (0, 0)),
            pl.BlockSpec((1, 1, BLOCK_PAD), lambda b: (b, 0, 0)),
            pl.BlockSpec((1, 1, BLOCK_PAD), lambda b: (b, 0, 0)),
            pl.BlockSpec(x.shape, lambda b: (0, 0)),
        ],
        out_specs=pl.BlockSpec((1, rows, BLOCK_PAD), lambda b: (b, 0, 0)),
        compiler_params=pltpu.CompilerParams(vmem_limit_bytes=40 * 2**20),
        name="sphere_select",
    )(column, kxy, kz, x)


def densities_of(occ_all, emp_all, occ_energy, emp_energy, gvec):
    weight = jnp.sqrt(4.0 / (emp_energy[None, :] - occ_energy[:, None])) / math.sqrt(GRID**3)
    x = compact(weight, occ_all, emp_all)
    rows = 2 * x.shape[1] * x.shape[2]
    return select(gvec, x.reshape(rows * KZ, 2 * HALF))


def body(occupied, empty, occ_energy, emp_energy, gvec):
    emp_all = lax.all_gather(empty, "occ", axis=2, tiled=True)
    occ_all = lax.all_gather(occupied, "emp", axis=2, tiled=True)
    d = densities_of(occ_all, emp_all, occ_energy, emp_energy, gvec)
    n_occ = lax.axis_size("occ")
    n_emp = lax.axis_size("emp")
    rows = d.shape[1]
    r = d.reshape(n_occ, 1, 2, rows, BLOCK_PAD)
    r = lax.all_to_all(r, "occ", split_axis=0, concat_axis=1, tiled=False) if False else lax.all_to_all(
        d.reshape(n_occ, 2, rows, BLOCK_PAD), "occ", split_axis=0, concat_axis=0, tiled=True
    )
    r = lax.all_gather(r, "emp", axis=0)
    c = lax.all_to_all(d, "emp", split_axis=0, concat_axis=0, tiled=True)
    c = lax.all_gather(c, "occ", axis=0)
    c = c.transpose(1, 0, 2, 3)
    half = rows // 2
    count = n_occ * n_emp * half
    factor = -1.0 / math.sqrt(count)
    cr, ci = c[:, :, :half], c[:, :, half:]
    turned = jnp.concatenate([-ci, cr], axis=2)
    dims = (((0, 1, 2), (0, 1, 2)), ((), ()))
    left = r.transpose(0, 1, 3, 2, 4)
    real = lax.dot_general(left, c, dims, preferred_element_type=f32)
    imag = lax.dot_general(left, turned, dims, preferred_element_type=f32)

    def trim(a):
        return (a * factor)[:, :BLOCK, :BLOCK].reshape(2 * BLOCK, BLOCK)

    return jnp.stack([trim(real), trim(imag)])


def solution(mesh):
    placed = (P(None, "occ", "emp", None), P(None, "emp", "occ", None), P("occ"), P("emp"), P())
    return jax.shard_map(
        body, mesh=mesh, in_specs=placed, out_specs=P(None, "occ", "emp"), check_vma=False
    )
```

```python
import functools
import math

import jax
import jax.numpy as jnp
import ml_dtypes
import numpy as np
from jax import lax
from jax.experimental import pallas as pl
from jax.experimental.pallas import tpu as pltpu
from jax.sharding import PartitionSpec as P

GRID = 96
KB = 25
REACH = KB // 2
NG = 8000
RSQ = 153
GROUPS = 24
SLAB = 6
ROWS = GROUPS * SLAB
HALF = 256
KZ = 32
BLOCK = 500
BLOCK_PAD = 512

f32 = jnp.float32
bf16 = jnp.bfloat16


def split(table):
    high = table.astype(ml_dtypes.bfloat16)
    low = (table - high.astype(np.float64)).astype(ml_dtypes.bfloat16)
    return high, low


def half_disc():
    kept = []
    for kx in range(-REACH, REACH + 1):
        for ky in range(-REACH, REACH + 1):
            if kx * kx + ky * ky <= RSQ and (kx > 0 or (kx == 0 and ky >= 0)):
                kept.append((kx, ky))
    return np.array(kept)


def tables():
    theta = 2.0 * np.pi / GRID
    disc = half_disc()
    kx, ky = disc[:, 0], disc[:, 1]
    freq = (np.arange(KB) + REACH) % KB - REACH
    angle = theta * (np.outer(np.arange(GRID), freq) % GRID)
    first = np.zeros((2, 4, GRID, 2, 4, KZ))
    for y in range(4):
        first[0, y, :, 0, y, :KB] = np.cos(angle)
        first[0, y, :, 1, y, :KB] = -np.sin(angle)
        first[1, y, :, 0, y, :KB] = np.sin(angle)
        first[1, y, :, 1, y, :KB] = np.cos(angle)
    first = first.reshape(768, 256)
    half, slab, j, x = [a.reshape(-1) for a in np.meshgrid(*map(np.arange, (2, 8, GROUPS, SLAB)), indexing="ij")]
    x = 2 * SLAB * slab + SLAB * half + x
    angle = theta * ((np.outer(kx, x) + 4 * np.outer(ky, j)) % GRID)
    second = np.zeros((2, HALF, GROUPS * GRID))
    second[0, : len(disc)] = np.cos(angle)
    second[1, : len(disc)] = np.sin(angle)
    second = second.reshape(2 * HALF, GROUPS * GRID)
    angle = theta * ((ky[:, None] * np.repeat(np.arange(4), KZ)[None, :]) % GRID)
    twiddle = np.zeros((2, HALF, 4 * KZ), np.float32)
    twiddle[0, : len(disc)] = np.cos(angle)
    twiddle[1, : len(disc)] = np.sin(angle)
    column = np.full((2, HALF), -1, np.int32)
    column[0, : len(disc)] = (kx % KB) * KB + ky % KB
    column[1, 1 : len(disc)] = ((-kx) % KB)[1:] * KB + ((-ky) % KB)[1:]
    return split(first), split(second), twiddle, column.reshape(2 * HALF, 1)


MESH = pl.DeviceIdType.MESH
KINDS = 9


def gather_steps(send, recv, shard, piece, hi, ring, device_of):
    own = hi * 4 + ring
    mate = (1 - hi) * 4 + ring
    right, left, far = lax.rem(ring + 1, 4), lax.rem(ring + 3, 4), lax.rem(ring + 2, 4)

    def copy(kind, ref, target):
        return pltpu.make_async_remote_copy(
            src_ref=ref,
            dst_ref=ref,
            send_sem=send.at[kind],
            recv_sem=recv.at[kind],
            device_id=device_of(target),
            device_id_type=MESH,
        )

    to_right, to_left = hi * 4 + right, hi * 4 + left
    from_left, from_right, across = hi * 4 + left, hi * 4 + right, hi * 4 + far
    mate_left, mate_right, mate_across = (1 - hi) * 4 + left, (1 - hi) * 4 + right, (1 - hi) * 4 + far

    sends = [
        (0, shard(own), mate),
        (1, shard(own), to_right),
        (2, shard(own), to_left),
        (3, shard(mate), to_right),
        (4, shard(mate), to_left),
        (5, piece(from_left, 0), to_right),
        (6, piece(from_right, 1), to_left),
        (7, piece(mate_left, 0), to_right),
        (8, piece(mate_right, 1), to_left),
    ]
    landings = [
        shard(mate),
        shard(from_left),
        shard(from_right),
        shard(mate_left),
        shard(mate_right),
        piece(across, 0),
        piece(across, 1),
        piece(mate_across, 0),
        piece(mate_across, 1),
    ]

    def start(*kinds):
        for kind in kinds:
            copy(*sends[kind]).start()

    def arrived(*kinds):
        for kind in kinds:
            copy(kind, landings[kind], own).wait_recv()

    def begin():
        start(0, 1, 2)

    def mid():
        arrived(0)
        start(3, 4)
        arrived(1)
        start(5)
        arrived(2)
        start(6)

    def late():
        arrived(3)
        start(7)
        arrived(4)
        start(8)

    def finish():
        arrived(5, 6, 7, 8)

    def sent():
        for kind in range(KINDS):
            copy(*sends[kind]).wait_send()

    return begin, mid, late, finish, sent


def pair_kernel(
    weight, occ_in, emp_in, t_hi, t_lo, a_hi, a_lo, tw, out,
    occ, emp, z_hi, z_lo, local, o_send, o_recv, e_send, e_recv, s_send, s_recv,
):
    n_occ, n_emp = occ.shape[0], emp.shape[0]
    o = lax.axis_index("occ")
    m = lax.axis_index("emp")
    o_hi, o_ring = o // 4, lax.rem(o, 4)
    chip, core = m // 2, lax.rem(m, 2)
    c_hi, c_ring = chip // 4, lax.rem(chip, 4)

    def emp_band(c):
        return gather_steps(
            e_send.at[c], e_recv.at[c],
            lambda i: emp.at[c, :, i],
            lambda i, h: emp.at[c, h, i],
            o_hi, o_ring,
            lambda i: {"occ": i, "emp": m},
        )

    def occ_band(v):
        return gather_steps(
            o_send.at[v], o_recv.at[v],
            lambda i: occ.at[v, core, i],
            lambda i, h: occ.at[v, core, i, h],
            c_hi, c_ring,
            lambda i: {"occ": o, "emp": 2 * i + core},
        )

    sibling = {"occ": o, "emp": 2 * chip + 1 - core}

    def share(v, mine):
        return pltpu.make_async_remote_copy(
            src_ref=occ.at[v, mine],
            dst_ref=occ.at[v, mine],
            send_sem=s_send.at[v],
            recv_sem=s_recv.at[v],
            device_id=sibling,
            device_id_type=MESH,
        )

    copies = []
    for v in range(n_occ):
        copies.append(pltpu.make_async_copy(occ_in.at[v], occ.at[v, core, chip], local.at[v]))
    for c in range(n_emp):
        copies.append(pltpu.make_async_copy(emp_in.at[c], emp.at[c, :, o], local.at[n_occ + c]))
    for copy in copies:
        copy.start()

    barrier = pltpu.get_barrier_semaphore()
    peers = [
        {"occ": (1 - o_hi) * 4 + o_ring, "emp": m},
        {"occ": o_hi * 4 + lax.rem(o_ring + 1, 4), "emp": m},
        {"occ": o_hi * 4 + lax.rem(o_ring + 3, 4), "emp": m},
        {"occ": o, "emp": 2 * ((1 - c_hi) * 4 + c_ring) + core},
        {"occ": o, "emp": 2 * (c_hi * 4 + lax.rem(c_ring + 1, 4)) + core},
        {"occ": o, "emp": 2 * (c_hi * 4 + lax.rem(c_ring + 3, 4)) + core},
        sibling,
    ]
    for peer in peers:
        pl.semaphore_signal(barrier, inc=1, device_id=peer, device_id_type=MESH)
    pl.semaphore_wait(barrier, len(peers))
    for copy in copies:
        copy.wait()

    E = [emp_band(c) for c in range(n_emp)]
    O = [occ_band(v) for v in range(n_occ)]
    BEGIN, MID, LATE, FINISH, SENT = range(5)

    def pass_on(v):
        O[v][FINISH]()
        share(v, core).start()

    def shared(v):
        share(v, 1 - core).wait_recv()

    E[0][BEGIN]()
    O[0][BEGIN]()
    O[1][BEGIN]()
    O[0][MID]()
    E[0][MID]()
    O[0][LATE]()
    E[0][LATE]()
    E[1][BEGIN]()
    O[1][MID]()
    O[2][BEGIN]()
    O[1][LATE]()
    O[3][BEGIN]()
    pass_on(0)
    O[2][MID]()
    E[0][FINISH]()
    shared(0)

    steps = {
        1: (O[2][LATE], O[3][MID], E[1][MID], lambda: pass_on(1), lambda: shared(1)),
        2: (O[3][LATE], E[1][LATE], E[2][BEGIN], lambda: pass_on(2), lambda: shared(2)),
        3: (lambda: pass_on(3), lambda: shared(3)),
        4: (E[1][FINISH], E[2][MID], E[3][BEGIN]),
        5: (E[2][LATE],),
        6: (E[3][MID],),
        7: (E[3][LATE],),
        8: (E[2][FINISH],),
        12: (E[3][FINISH],),
    }
    tile = TILE

    def one_pair(n, carry):
        c = n // n_occ
        v = lax.rem(n, n_occ)
        for step, actions in steps.items():

            @pl.when(n == step)
            def _(actions=actions):
                for action in actions:
                    action()

        def one_tile(t, carry2):
            high_rows = []
            low_rows = []
            for i in range(tile):
                slab = t * tile + i
                h, s = slab // 8, lax.rem(slab, 8)
                real = []
                imag = []
                for q in range(3):
                    vr = occ[v, h, s, 0, q].astype(f32)
                    vi = occ[v, h, s, 1, q].astype(f32)
                    cr = emp[c, h, s, 0, q].astype(f32)
                    ci = emp[c, h, s, 1, q].astype(f32)
                    real.append(vr * cr + vi * ci)
                    imag.append(vr * ci - vi * cr)
                parts = real + imag
                high = [p.astype(bf16) for p in parts]
                low = [(p - h_.astype(f32)).astype(bf16) for p, h_ in zip(parts, high)]
                high_rows.append(jnp.concatenate(high, axis=1))
                low_rows.append(jnp.concatenate(low, axis=1))
            high = jnp.concatenate(high_rows, axis=0)
            low = jnp.concatenate(low_rows, axis=0)
            z = (
                jnp.dot(high, t_hi[...], preferred_element_type=f32)
                + jnp.dot(low, t_hi[...], preferred_element_type=f32)
                + jnp.dot(high, t_lo[...], preferred_element_type=f32)
            )
            zh = z.astype(bf16)
            where = pl.ds(pl.multiple_of(t * (tile * ROWS), 16), tile * ROWS)
            z_hi[where, :] = zh
            z_lo[where, :] = (z - zh.astype(f32)).astype(bf16)
            return carry2

        lax.fori_loop(0, 16 // tile, one_tile, 0)
        both = (
            jnp.dot(a_hi[...], z_hi[...], preferred_element_type=f32)
            + jnp.dot(a_hi[...], z_lo[...], preferred_element_type=f32)
            + jnp.dot(a_lo[...], z_hi[...], preferred_element_type=f32)
        )
        ur = both[:HALF, :128]
        ui = both[:HALF, 128:]
        wr = both[HALF:, :128]
        wi = both[HALF:, 128:]
        cos, sin = tw[0], tw[1]
        w = weight[v, c]
        for sign in range(2):
            s = 1.0 - 2.0 * sign
            pr = ur + s * wi
            pi = ui - s * wr
            qr = (cos * pr + s * (sin * pi)).T
            qi = (cos * pi - s * (sin * pr)).T
            for at, q in ((0, qr), (1, qi)):
                total = (q[:KZ] + q[KZ : 2 * KZ]) + (q[2 * KZ : 3 * KZ] + q[3 * KZ :])
                out[at, v, c, :, sign * HALF : (sign + 1) * HALF] = (total * w).astype(bf16)
        return carry

    lax.fori_loop(0, n_occ * n_emp, one_pair, 0)
    for v in range(n_occ):
        O[v][SENT]()
        share(v, core).wait_send()
    for c in range(n_emp):
        E[c][SENT]()


TILE = 4


def compact(weight, occupied, empty):
    (t_hi, t_lo), (a_hi, a_lo), tw, unused = tables()
    n_occ, n_emp = occupied.shape[1], empty.shape[1]
    occ_in = occupied.reshape(2, n_occ, SLAB, GROUPS, 3, 128).transpose(1, 0, 4, 3, 2, 5)
    occ_in = occ_in.reshape(n_occ, 2, 3, ROWS, 128)
    emp_in = empty.reshape(2, n_emp, 2, SLAB, GROUPS, 3, 128).transpose(1, 2, 0, 5, 4, 3, 6)
    emp_in = emp_in.reshape(n_emp, 2, 2, 3, ROWS, 128)
    vmem = pl.BlockSpec(memory_space=pltpu.VMEM)
    hbm = pl.BlockSpec(memory_space=pl.ANY)
    dma = pltpu.SemaphoreType.DMA
    return pl.pallas_call(
        pair_kernel,
        out_shape=jax.ShapeDtypeStruct((2, n_occ, n_emp, KZ, 2 * HALF), bf16),
        in_specs=[pl.BlockSpec(memory_space=pltpu.SMEM), hbm, hbm] + [vmem] * 5,
        out_specs=vmem,
        scratch_shapes=[
            pltpu.VMEM((n_occ, 2, 8, 2, 3, ROWS, 128), bf16),
            pltpu.VMEM((n_emp, 2, 8, 2, 3, ROWS, 128), bf16),
            pltpu.VMEM((GROUPS * GRID, 256), bf16),
            pltpu.VMEM((GROUPS * GRID, 256), bf16),
            dma((n_occ + n_emp,)),
            dma((n_occ, KINDS)),
            dma((n_occ, KINDS)),
            dma((n_emp, KINDS)),
            dma((n_emp, KINDS)),
            dma((n_occ,)),
            dma((n_occ,)),
        ],
        compiler_params=pltpu.CompilerParams(
            vmem_limit_bytes=60 * 2**20, collective_id=0, has_side_effects=True
        ),
        name="pair_spectra",
    )(weight, occ_in, emp_in, t_hi, t_lo, a_hi, a_lo, tw)


def select_kernel(column, kxy, kz, x, out):
    hot = jnp.where(column[...] == kxy[0], 1.0, 0.0).astype(bf16)
    rows = x.shape[0] // KZ
    picked = jnp.dot(x[...], hot, preferred_element_type=f32)
    level = lax.broadcasted_iota(jnp.int32, (KZ, BLOCK_PAD), 0)
    mask = jnp.where(level == kz[0], 1.0, 0.0)
    total = jnp.sum(picked.reshape(rows, KZ, BLOCK_PAD) * mask[None], axis=1)
    out[0] = total.astype(bf16)


def select(gvec, x):
    column = tables()[3]
    blocks = NG // BLOCK
    padded = jnp.pad(gvec.reshape(blocks, 1, BLOCK), ((0, 0), (0, 0), (0, BLOCK_PAD - BLOCK)), constant_values=0)
    kxy = padded // KB
    kz = padded - kxy * KB
    live = lax.broadcasted_iota(jnp.int32, padded.shape, 2) < BLOCK
    kxy = jnp.where(live, kxy, -2)
    rows = x.shape[0] // KZ
    return pl.pallas_call(
        select_kernel,
        grid=(blocks,),
        out_shape=jax.ShapeDtypeStruct((blocks, rows, BLOCK_PAD), bf16),
        in_specs=[
            pl.BlockSpec((2 * HALF, 1), lambda b: (0, 0)),
            pl.BlockSpec((1, 1, BLOCK_PAD), lambda b: (b, 0, 0)),
            pl.BlockSpec((1, 1, BLOCK_PAD), lambda b: (b, 0, 0)),
            pl.BlockSpec(x.shape, lambda b: (0, 0)),
        ],
        out_specs=pl.BlockSpec((1, rows, BLOCK_PAD), lambda b: (b, 0, 0)),
        compiler_params=pltpu.CompilerParams(vmem_limit_bytes=40 * 2**20),
        name="sphere_select",
    )(column, kxy, kz, x)


def densities_of(occ_all, emp_all, occ_energy, emp_energy, gvec):
    weight = jnp.sqrt(4.0 / (emp_energy[None, :] - occ_energy[:, None])) / math.sqrt(GRID**3)
    x = compact(weight, occ_all, emp_all)
    rows = 2 * x.shape[1] * x.shape[2]
    return select(gvec, x.reshape(rows * KZ, 2 * HALF))


def body(occupied, empty, occ_energy, emp_energy, gvec):
    d = densities_of(occupied, empty, occ_energy, emp_energy, gvec)
    n_occ = lax.axis_size("occ")
    n_emp = lax.axis_size("emp")
    rows = d.shape[1]
    r = lax.all_to_all(d.reshape(n_occ, 2, rows, BLOCK_PAD), "occ", split_axis=0, concat_axis=0, tiled=True)
    r = lax.all_gather(r, "emp", axis=0)
    c = lax.all_to_all(d, "emp", split_axis=0, concat_axis=0, tiled=True)
    c = lax.all_gather(c, "occ", axis=0)
    c = c.transpose(1, 0, 2, 3)
    half = rows // 2
    count = n_occ * n_emp * half
    factor = -1.0 / math.sqrt(count)
    cr, ci = c[:, :, :half], c[:, :, half:]
    turned = jnp.concatenate([-ci, cr], axis=2)
    dims = (((0, 1, 2), (0, 1, 2)), ((), ()))
    left = r.transpose(0, 1, 3, 2, 4)
    real = lax.dot_general(left, c, dims, preferred_element_type=f32)
    imag = lax.dot_general(left, turned, dims, preferred_element_type=f32)

    def trim(a):
        return (a * factor)[:, :BLOCK, :BLOCK].reshape(2 * BLOCK, BLOCK)

    return jnp.stack([trim(real), trim(imag)])


def solution(mesh):
    placed = (P(None, "occ", "emp", None), P(None, "emp", "occ", None), P("occ"), P("emp"), P())
    return jax.shard_map(
        body, mesh=mesh, in_specs=placed, out_specs=P(None, "occ", "emp"), check_vma=False
    )
```

```python
import functools
import math

import jax
import jax.numpy as jnp
import ml_dtypes
import numpy as np
from jax import lax
from jax.experimental import pallas as pl
from jax.experimental.pallas import tpu as pltpu
from jax.sharding import PartitionSpec as P

GRID = 96
KB = 25
REACH = KB // 2
NG = 8000
RSQ = 153
GROUPS = 24
SLAB = 6
ROWS = GROUPS * SLAB
HALF = 256
KZ = 32
BLOCK = 500
BLOCK_PAD = 512

f32 = jnp.float32
bf16 = jnp.bfloat16


def split(table):
    high = table.astype(ml_dtypes.bfloat16)
    low = (table - high.astype(np.float64)).astype(ml_dtypes.bfloat16)
    return high, low


def half_disc():
    kept = []
    for kx in range(-REACH, REACH + 1):
        for ky in range(-REACH, REACH + 1):
            if kx * kx + ky * ky <= RSQ and (kx > 0 or (kx == 0 and ky >= 0)):
                kept.append((kx, ky))
    return np.array(kept)


def tables():
    theta = 2.0 * np.pi / GRID
    disc = half_disc()
    kx, ky = disc[:, 0], disc[:, 1]
    freq = (np.arange(KB) + REACH) % KB - REACH
    angle = theta * (np.outer(np.arange(GRID), freq) % GRID)
    first = np.zeros((2, 4, GRID, 2, 4, KZ))
    for y in range(4):
        first[0, y, :, 0, y, :KB] = np.cos(angle)
        first[0, y, :, 1, y, :KB] = -np.sin(angle)
        first[1, y, :, 0, y, :KB] = np.sin(angle)
        first[1, y, :, 1, y, :KB] = np.cos(angle)
    first = first.reshape(768, 256)
    half, slab, j, x = [a.reshape(-1) for a in np.meshgrid(*map(np.arange, (2, 8, GROUPS, SLAB)), indexing="ij")]
    x = 2 * SLAB * slab + SLAB * half + x
    angle = theta * ((np.outer(kx, x) + 4 * np.outer(ky, j)) % GRID)
    second = np.zeros((2, HALF, GROUPS * GRID))
    second[0, : len(disc)] = np.cos(angle)
    second[1, : len(disc)] = np.sin(angle)
    second = second.reshape(2 * HALF, GROUPS * GRID)
    angle = theta * ((ky[:, None] * np.repeat(np.arange(4), KZ)[None, :]) % GRID)
    twiddle = np.zeros((2, HALF, 4 * KZ), np.float32)
    twiddle[0, : len(disc)] = np.cos(angle)
    twiddle[1, : len(disc)] = np.sin(angle)
    column = np.full((2, HALF), -1, np.int32)
    column[0, : len(disc)] = (kx % KB) * KB + ky % KB
    column[1, 1 : len(disc)] = ((-kx) % KB)[1:] * KB + ((-ky) % KB)[1:]
    return split(first), split(second), twiddle, column.reshape(2 * HALF, 1)


MESH = pl.DeviceIdType.MESH
KINDS = 9


def gather_steps(send, recv, shard, piece, hi, ring, device_of, landed=lambda i: None):
    own = hi * 4 + ring
    mate = (1 - hi) * 4 + ring
    right, left, far = lax.rem(ring + 1, 4), lax.rem(ring + 3, 4), lax.rem(ring + 2, 4)

    def copy(kind, ref, target):
        return pltpu.make_async_remote_copy(
            src_ref=ref,
            dst_ref=ref,
            send_sem=send.at[kind],
            recv_sem=recv.at[kind],
            device_id=device_of(target),
            device_id_type=MESH,
        )

    to_right, to_left = hi * 4 + right, hi * 4 + left
    from_left, from_right, across = hi * 4 + left, hi * 4 + right, hi * 4 + far
    mate_left, mate_right, mate_across = (1 - hi) * 4 + left, (1 - hi) * 4 + right, (1 - hi) * 4 + far

    sends = [
        (0, shard(own), mate),
        (1, shard(own), to_right),
        (2, shard(own), to_left),
        (3, shard(mate), to_right),
        (4, shard(mate), to_left),
        (5, piece(from_left, 0), to_right),
        (6, piece(from_right, 1), to_left),
        (7, piece(mate_left, 0), to_right),
        (8, piece(mate_right, 1), to_left),
    ]
    landings = [
        shard(mate),
        shard(from_left),
        shard(from_right),
        shard(mate_left),
        shard(mate_right),
        piece(across, 0),
        piece(across, 1),
        piece(mate_across, 0),
        piece(mate_across, 1),
    ]

    def start(*kinds):
        for kind in kinds:
            copy(*sends[kind]).start()

    def arrived(*kinds):
        for kind in kinds:
            copy(kind, landings[kind], own).wait_recv()

    def begin():
        start(0, 1, 2)
        landed(own)

    def mid():
        arrived(0)
        start(3, 4)
        arrived(1)
        start(5)
        arrived(2)
        start(6)
        landed(mate)
        landed(from_left)
        landed(from_right)

    def late():
        arrived(3)
        start(7)
        arrived(4)
        start(8)
        landed(mate_left)
        landed(mate_right)

    def finish():
        arrived(5, 6, 7, 8)
        landed(across)
        landed(mate_across)

    def sent():
        for kind in range(KINDS):
            copy(*sends[kind]).wait_send()

    return begin, mid, late, finish, sent


def pair_kernel(
    weight, occ_in, emp_in, t_hi, t_lo, a_hi, a_lo, tw, out,
    occ, emp, z_hi, z_lo, local, o_send, o_recv, e_send, e_recv, s_send, s_recv,
):
    n_occ, n_emp = occ.shape[0], emp.shape[0]
    o = lax.axis_index("occ")
    m = lax.axis_index("emp")
    o_hi, o_ring = o // 4, lax.rem(o, 4)
    chip, core = m // 2, lax.rem(m, 2)
    c_hi, c_ring = chip // 4, lax.rem(chip, 4)

    def emp_band(c):
        return gather_steps(
            e_send.at[c], e_recv.at[c],
            lambda i: emp.at[c, :, i],
            lambda i, h: emp.at[c, h, i],
            o_hi, o_ring,
            lambda i: {"occ": i, "emp": m},
        )

    def occ_band(v):
        return gather_steps(
            o_send.at[v], o_recv.at[v],
            lambda i: occ.at[v, core, i],
            lambda i, h: occ.at[v, core, i, h],
            c_hi, c_ring,
            lambda i: {"occ": o, "emp": 2 * i + core},
        )

    sibling = {"occ": o, "emp": 2 * chip + 1 - core}

    def share(v, mine):
        return pltpu.make_async_remote_copy(
            src_ref=occ.at[v, mine],
            dst_ref=occ.at[v, mine],
            send_sem=s_send.at[v],
            recv_sem=s_recv.at[v],
            device_id=sibling,
            device_id_type=MESH,
        )

    copies = []
    for v in range(n_occ):
        copies.append(pltpu.make_async_copy(occ_in.at[v], occ.at[v, core, chip], local.at[v]))
    for c in range(n_emp):
        copies.append(pltpu.make_async_copy(emp_in.at[c], emp.at[c, :, o], local.at[n_occ + c]))
    for copy in copies:
        copy.start()

    barrier = pltpu.get_barrier_semaphore()
    peers = [
        {"occ": (1 - o_hi) * 4 + o_ring, "emp": m},
        {"occ": o_hi * 4 + lax.rem(o_ring + 1, 4), "emp": m},
        {"occ": o_hi * 4 + lax.rem(o_ring + 3, 4), "emp": m},
        {"occ": o, "emp": 2 * ((1 - c_hi) * 4 + c_ring) + core},
        {"occ": o, "emp": 2 * (c_hi * 4 + lax.rem(c_ring + 1, 4)) + core},
        {"occ": o, "emp": 2 * (c_hi * 4 + lax.rem(c_ring + 3, 4)) + core},
        sibling,
    ]
    for peer in peers:
        pl.semaphore_signal(barrier, inc=1, device_id=peer, device_id_type=MESH)
    pl.semaphore_wait(barrier, len(peers))
    for copy in copies:
        copy.wait()

    E = [emp_band(c) for c in range(n_emp)]
    O = [occ_band(v) for v in range(n_occ)]

    def pass_on(v):
        O[v][FINISH]()
        share(v, core).start()

    def shared(v):
        share(v, 1 - core).wait_recv()

    E[0][BEGIN]()
    O[0][BEGIN]()
    O[1][BEGIN]()
    O[0][MID]()
    E[0][MID]()
    O[0][LATE]()
    E[0][LATE]()
    E[1][BEGIN]()
    O[1][MID]()
    O[2][BEGIN]()
    O[1][LATE]()
    O[3][BEGIN]()
    pass_on(0)
    O[2][MID]()
    E[0][FINISH]()
    shared(0)

    steps = {
        1: (O[2][LATE], O[3][MID], E[1][MID], lambda: pass_on(1), lambda: shared(1)),
        2: (O[3][LATE], E[1][LATE], E[2][BEGIN], lambda: pass_on(2), lambda: shared(2)),
        3: (lambda: pass_on(3), lambda: shared(3)),
        4: (E[1][FINISH], E[2][MID], E[3][BEGIN]),
        5: (E[2][LATE],),
        6: (E[3][MID],),
        7: (E[3][LATE],),
        8: (E[2][FINISH],),
        12: (E[3][FINISH],),
    }
    tile = TILE

    def one_pair(n, carry):
        c = n // n_occ
        v = lax.rem(n, n_occ)
        for step, actions in steps.items():

            @pl.when(n == step)
            def _(actions=actions):
                for action in actions:
                    action()

        def one_tile(t, carry2):
            high_rows = []
            low_rows = []
            for i in range(tile):
                slab = t * tile + i
                h, s = slab // 8, lax.rem(slab, 8)
                real = []
                imag = []
                for q in range(3):
                    vr = occ[v, h, s, 0, q].astype(f32)
                    vi = occ[v, h, s, 1, q].astype(f32)
                    cr = emp[c, h, s, 0, q].astype(f32)
                    ci = emp[c, h, s, 1, q].astype(f32)
                    real.append(vr * cr + vi * ci)
                    imag.append(vr * ci - vi * cr)
                parts = real + imag
                high = [p.astype(bf16) for p in parts]
                low = [(p - h_.astype(f32)).astype(bf16) for p, h_ in zip(parts, high)]
                high_rows.append(jnp.concatenate(high, axis=1))
                low_rows.append(jnp.concatenate(low, axis=1))
            high = jnp.concatenate(high_rows, axis=0)
            low = jnp.concatenate(low_rows, axis=0)
            z = (
                jnp.dot(high, t_hi[...], preferred_element_type=f32)
                + jnp.dot(low, t_hi[...], preferred_element_type=f32)
                + jnp.dot(high, t_lo[...], preferred_element_type=f32)
            )
            zh = z.astype(bf16)
            where = pl.ds(pl.multiple_of(t * (tile * ROWS), 16), tile * ROWS)
            z_hi[where, :] = zh
            z_lo[where, :] = (z - zh.astype(f32)).astype(bf16)
            return carry2

        lax.fori_loop(0, 16 // tile, one_tile, 0)
        both = (
            jnp.dot(a_hi[...], z_hi[...], preferred_element_type=f32)
            + jnp.dot(a_hi[...], z_lo[...], preferred_element_type=f32)
            + jnp.dot(a_lo[...], z_hi[...], preferred_element_type=f32)
        )
        ur = both[:HALF, :128]
        ui = both[:HALF, 128:]
        wr = both[HALF:, :128]
        wi = both[HALF:, 128:]
        cos, sin = tw[0], tw[1]
        w = weight[v, c]
        for sign in range(2):
            s = 1.0 - 2.0 * sign
            pr = ur + s * wi
            pi = ui - s * wr
            qr = (cos * pr + s * (sin * pi)).T
            qi = (cos * pi - s * (sin * pr)).T
            for at, q in ((0, qr), (1, qi)):
                total = (q[:KZ] + q[KZ : 2 * KZ]) + (q[2 * KZ : 3 * KZ] + q[3 * KZ :])
                out[at, v, c, :, sign * HALF : (sign + 1) * HALF] = (total * w).astype(bf16)
        return carry

    lax.fori_loop(0, n_occ * n_emp, one_pair, 0)
    for v in range(n_occ):
        O[v][SENT]()
        share(v, core).wait_send()
    for c in range(n_emp):
        E[c][SENT]()


TILE = 4


def compact(weight, occupied, empty):
    (t_hi, t_lo), (a_hi, a_lo), tw, unused = tables()
    n_occ, n_emp = occupied.shape[1], empty.shape[1]
    occ_in = occupied.reshape(2, n_occ, SLAB, GROUPS, 3, 128).transpose(1, 0, 4, 3, 2, 5)
    occ_in = occ_in.reshape(n_occ, 2, 3, ROWS, 128)
    emp_in = empty.reshape(2, n_emp, 2, SLAB, GROUPS, 3, 128).transpose(1, 2, 0, 5, 4, 3, 6)
    emp_in = emp_in.reshape(n_emp, 2, 2, 3, ROWS, 128)
    vmem = pl.BlockSpec(memory_space=pltpu.VMEM)
    hbm = pl.BlockSpec(memory_space=pl.ANY)
    dma = pltpu.SemaphoreType.DMA
    return pl.pallas_call(
        pair_kernel,
        out_shape=jax.ShapeDtypeStruct((2, n_occ, n_emp, KZ, 2 * HALF), bf16),
        in_specs=[pl.BlockSpec(memory_space=pltpu.SMEM), hbm, hbm] + [vmem] * 5,
        out_specs=vmem,
        scratch_shapes=[
            pltpu.VMEM((n_occ, 2, 8, 2, 3, ROWS, 128), bf16),
            pltpu.VMEM((n_emp, 2, 8, 2, 3, ROWS, 128), bf16),
            pltpu.VMEM((GROUPS * GRID, 256), bf16),
            pltpu.VMEM((GROUPS * GRID, 256), bf16),
            dma((n_occ + n_emp,)),
            dma((n_occ, KINDS)),
            dma((n_occ, KINDS)),
            dma((n_emp, KINDS)),
            dma((n_emp, KINDS)),
            dma((n_occ,)),
            dma((n_occ,)),
        ],
        compiler_params=pltpu.CompilerParams(
            vmem_limit_bytes=60 * 2**20, collective_id=0, has_side_effects=True
        ),
        name="pair_spectra",
    )(weight, occ_in, emp_in, t_hi, t_lo, a_hi, a_lo, tw)


def select_kernel(column, kxy, kz, x, out):
    hot = jnp.where(column[...] == kxy[0], 1.0, 0.0).astype(bf16)
    rows = x.shape[0] // KZ
    picked = jnp.dot(x[...], hot, preferred_element_type=f32)
    level = lax.broadcasted_iota(jnp.int32, (KZ, BLOCK_PAD), 0)
    mask = jnp.where(level == kz[0], 1.0, 0.0)
    total = jnp.sum(picked.reshape(rows, KZ, BLOCK_PAD) * mask[None], axis=1)
    out[0] = total.astype(bf16)


def select(gvec, x):
    column = tables()[3]
    blocks = NG // BLOCK
    padded = jnp.pad(gvec.reshape(blocks, 1, BLOCK), ((0, 0), (0, 0), (0, BLOCK_PAD - BLOCK)), constant_values=0)
    kxy = padded // KB
    kz = padded - kxy * KB
    live = lax.broadcasted_iota(jnp.int32, padded.shape, 2) < BLOCK
    kxy = jnp.where(live, kxy, -2)
    rows = x.shape[0] // KZ
    return pl.pallas_call(
        select_kernel,
        grid=(blocks,),
        out_shape=jax.ShapeDtypeStruct((blocks, rows, BLOCK_PAD), bf16),
        in_specs=[
            pl.BlockSpec((2 * HALF, 1), lambda b: (0, 0)),
            pl.BlockSpec((1, 1, BLOCK_PAD), lambda b: (b, 0, 0)),
            pl.BlockSpec((1, 1, BLOCK_PAD), lambda b: (b, 0, 0)),
            pl.BlockSpec(x.shape, lambda b: (0, 0)),
        ],
        out_specs=pl.BlockSpec((1, rows, BLOCK_PAD), lambda b: (b, 0, 0)),
        compiler_params=pltpu.CompilerParams(vmem_limit_bytes=40 * 2**20),
        name="sphere_select",
    )(column, kxy, kz, x)


def densities_of(occ_all, emp_all, occ_energy, emp_energy, gvec):
    weight = jnp.sqrt(4.0 / (emp_energy[None, :] - occ_energy[:, None])) / math.sqrt(GRID**3)
    x = compact(weight, occ_all, emp_all)
    rows = 2 * x.shape[1] * x.shape[2]
    return select(gvec, x.reshape(rows * KZ, 2 * HALF))


BEGIN, MID, LATE, FINISH, SENT = range(5)


def chi_kernel(factor, d, out, rows, cols, local, r_send, r_recv, c_send, c_recv, g_send, g_recv, s_send, s_recv):
    o = lax.axis_index("occ")
    m = lax.axis_index("emp")
    o_hi, o_ring = o // 4, lax.rem(o, 4)
    chip, core = m // 2, lax.rem(m, 2)
    c_hi, c_ring = chip // 4, lax.rem(chip, 4)

    def copy(src, dst, send, recv, device):
        return pltpu.make_async_remote_copy(
            src_ref=src, dst_ref=dst, send_sem=send, recv_sem=recv, device_id=device, device_id_type=MESH
        )

    own_copies = [pltpu.make_async_copy(d.at[2 * o + b], rows.at[b, core, o, chip], local.at[b]) for b in range(2)]
    own_copies.append(pltpu.make_async_copy(d.at[m], cols.at[core, o, chip], local.at[2]))
    for own_copy in own_copies:
        own_copy.start()

    barrier = pltpu.get_barrier_semaphore()
    for step in range(1, 8):
        peer = {"occ": lax.rem(o + step, 8), "emp": m}
        pl.semaphore_signal(barrier, inc=1, device_id=peer, device_id_type=MESH)
    for step in range(1, 16):
        peer = {"occ": o, "emp": lax.rem(m + step, 16)}
        pl.semaphore_signal(barrier, inc=1, device_id=peer, device_id_type=MESH)
    pl.semaphore_wait(barrier, 22)

    def row_part(b, step):
        to = lax.rem(o + step, 8)
        return copy(
            d.at[2 * to + b], rows.at[b, core, o, chip], r_send.at[b, step - 1], r_recv.at[b, step - 1],
            {"occ": to, "emp": m},
        )

    def row_landing(b, step):
        here = rows.at[b, core, lax.rem(o + 8 - step, 8), chip]
        return copy(here, here, r_send.at[b, step - 1], r_recv.at[b, step - 1], {"occ": o, "emp": m})

    def col_part(step):
        to = lax.rem(m + step, 16)
        return copy(
            d.at[to], cols.at[core, o, chip], c_send.at[step - 1], c_recv.at[step - 1], {"occ": o, "emp": to}
        )

    def col_landing(step):
        source = lax.rem(m + 16 - step, 16)
        here = cols.at[lax.rem(source, 2), o, source // 2]
        return copy(here, here, c_send.at[step - 1], c_recv.at[step - 1], {"occ": o, "emp": m})

    row_steps = range(1, 8)
    even, odd = range(2, 16, 2), range(1, 16, 2)
    for step in row_steps:
        row_part(0, step).start()
    for step in even:
        col_part(step).start()
    for step in row_steps:
        row_part(1, step).start()
    for step in odd:
        col_part(step).start()

    sibling = {"occ": o, "emp": 2 * chip + 1 - core}

    def share(b, mine, i):
        here = rows.at[b, mine, :, i]
        return copy(here, here, s_send.at[b, i], s_recv.at[b, i], sibling)

    def row_band(b):
        return gather_steps(
            g_send.at[b], g_recv.at[b],
            lambda i: rows.at[b, core, :, i],
            lambda i, h: rows.at[b, core, pl.ds(4 * h, 4), i],
            c_hi, c_ring,
            lambda i: {"occ": o, "emp": 2 * i + core},
            lambda i: share(b, core, i).start(),
        )

    def col_band(j):
        k = core if j == 0 else 1 - core
        return gather_steps(
            g_send.at[2 + j], g_recv.at[2 + j],
            lambda i: cols.at[k, i],
            lambda i, h: cols.at[k, i, pl.ds(4 * h, 4)],
            o_hi, o_ring,
            lambda i: {"occ": i, "emp": m},
        )

    R = [row_band(b) for b in range(2)]
    C = [col_band(j) for j in range(2)]
    for own_copy in own_copies:
        own_copy.wait()
    for step in row_steps:
        row_landing(0, step).wait_recv()
    R[0][BEGIN]()
    for step in even:
        col_landing(step).wait_recv()
    C[0][BEGIN]()
    for step in row_steps:
        row_landing(1, step).wait_recv()
    R[1][BEGIN]()
    for step in odd:
        col_landing(step).wait_recv()
    C[1][BEGIN]()
    for part in (MID, LATE, FINISH):
        for band in (R[0], C[0], R[1], C[1]):
            band[part]()

    depth = rows.shape[2] * rows.shape[3] * rows.shape[4]
    half = rows.shape[4] // 2

    def multiply(k, last):
        right = cols[k].reshape(depth // (2 * half), 2 * half, BLOCK_PAD)
        turned = jnp.concatenate([-right[:, half:], right[:, :half]], axis=1)
        right = right.reshape(depth, BLOCK_PAD)
        turned = turned.reshape(depth, BLOCK_PAD)
        for b in range(2):
            left = rows[b, k].reshape(depth, BLOCK_PAD)
            for at, side in ((0, right), (1, turned)):
                part = lax.dot_general(left, side, (((0,), (0,)), ((), ())), preferred_element_type=f32)
                out[at, b] = (out[at, b] + part) * factor if last else part

    multiply(core, False)
    for b in range(2):
        for i in range(8):
            share(b, 1 - core, i).wait_recv()
    multiply(1 - core, True)
    for step in row_steps:
        for b in range(2):
            row_part(b, step).wait_send()
    for step in range(1, 16):
        col_part(step).wait_send()
    for band in R + C:
        band[SENT]()
    for b in range(2):
        for i in range(8):
            share(b, core, i).wait_send()


def body(occupied, empty, occ_energy, emp_energy, gvec):
    d = densities_of(occupied, empty, occ_energy, emp_energy, gvec)
    rows = d.shape[1]
    n_occ = lax.axis_size("occ")
    n_emp = lax.axis_size("emp")
    factor = -1.0 / math.sqrt(n_occ * n_emp * (rows // 2))
    vmem = pl.BlockSpec(memory_space=pltpu.VMEM)
    dma = pltpu.SemaphoreType.DMA
    chi = pl.pallas_call(
        functools.partial(chi_kernel, factor),
        out_shape=jax.ShapeDtypeStruct((2, 2, BLOCK_PAD, BLOCK_PAD), f32),
        in_specs=[pl.BlockSpec(memory_space=pl.ANY)],
        out_specs=vmem,
        scratch_shapes=[
            pltpu.VMEM((2, 2, 8, 8, rows, BLOCK_PAD), bf16),
            pltpu.VMEM((2, 8, 8, rows, BLOCK_PAD), bf16),
            dma((3,)),
            dma((2, 7)),
            dma((2, 7)),
            dma((15,)),
            dma((15,)),
            dma((4, KINDS)),
            dma((4, KINDS)),
            dma((2, 8)),
            dma((2, 8)),
        ],
        compiler_params=pltpu.CompilerParams(
            vmem_limit_bytes=56 * 2**20, collective_id=1, has_side_effects=True
        ),
        name="chi_blocks",
    )(d)
    return chi[:, :, :BLOCK, :BLOCK].reshape(2, 2 * BLOCK, BLOCK)


def solution(mesh):
    placed = (P(None, "occ", "emp", None), P(None, "emp", "occ", None), P("occ"), P("emp"), P())
    return jax.shard_map(
        body, mesh=mesh, in_specs=placed, out_specs=P(None, "occ", "emp"), check_vma=False
    )
```

```python
import functools
import math

import jax
import jax.numpy as jnp
import ml_dtypes
import numpy as np
from jax import lax
from jax.experimental import pallas as pl
from jax.experimental.pallas import tpu as pltpu
from jax.sharding import PartitionSpec as P

GRID = 96
KB = 25
REACH = KB // 2
NG = 8000
RSQ = 153
GROUPS = 24
SLAB = 6
ROWS = GROUPS * SLAB
HALF = 256
KZ = 32
CHUNK_Y = ((0, 1), (2, 1), (2, 3))
RING_FIRST = ()
BLOCK = 500
BLOCK_PAD = 512

f32 = jnp.float32
bf16 = jnp.bfloat16


def split(table):
    high = table.astype(ml_dtypes.bfloat16)
    low = (table - high.astype(np.float64)).astype(ml_dtypes.bfloat16)
    return high, low


def half_disc():
    kept = []
    for kx in range(-REACH, REACH + 1):
        for ky in range(-REACH, REACH + 1):
            if kx * kx + ky * ky <= RSQ and (kx > 0 or (kx == 0 and ky >= 0)):
                kept.append((kx, ky))
    return np.array(kept)


def tables():
    theta = 2.0 * np.pi / GRID
    disc = half_disc()
    kx, ky = disc[:, 0], disc[:, 1]
    freq = (np.arange(KB) + REACH) % KB - REACH
    first = np.zeros((3, 2, 128, 2, 2, KZ))
    for q in range(3):
        for lane in range(128):
            y, z = divmod(q * 128 + lane, GRID)
            slot = CHUNK_Y[q].index(y)
            angle = theta * (z * freq % GRID)
            first[q, 0, lane, slot, 0, :KB] = np.cos(angle)
            first[q, 0, lane, slot, 1, :KB] = -np.sin(angle)
            first[q, 1, lane, slot, 0, :KB] = np.sin(angle)
            first[q, 1, lane, slot, 1, :KB] = np.cos(angle)
    first = first.reshape(768, 128)
    half, slab, j, x = [a.reshape(-1) for a in np.meshgrid(*map(np.arange, (2, 8, GROUPS, SLAB)), indexing="ij")]
    x = 2 * SLAB * slab + SLAB * half + x
    angle = theta * ((np.outer(kx, x) + 4 * np.outer(ky, j)) % GRID)
    second = np.zeros((2, HALF, GROUPS * GRID))
    second[0, : len(disc)] = np.cos(angle)
    second[1, : len(disc)] = np.sin(angle)
    second = second.reshape(2 * HALF, GROUPS * GRID)
    angle = theta * ((ky[:, None] * np.repeat(np.arange(4), 2 * KZ)[None, :]) % GRID)
    turn = np.tile(np.repeat([1.0, -1.0], KZ), 4)
    twiddle = np.zeros((2, HALF, 8 * KZ), np.float32)
    twiddle[0, : len(disc)] = np.cos(angle)
    twiddle[1, : len(disc)] = np.sin(angle) * turn
    column = np.full((2, HALF), -1, np.int32)
    column[0, : len(disc)] = (kx % KB) * KB + ky % KB
    column[1, 1 : len(disc)] = ((-kx) % KB)[1:] * KB + ((-ky) % KB)[1:]
    first_hi, first_lo = split(first)
    first = np.concatenate([first_hi, first_lo], axis=1)
    second = np.concatenate(split(second), axis=0)
    return first, second, twiddle, column.reshape(2 * HALF, 1)


MESH = pl.DeviceIdType.MESH
KINDS = 9


def gather_steps(send, recv, shard, piece, hi, ring, device_of, landed=lambda i: None, ring_first=False):
    own = hi * 4 + ring
    mate = (1 - hi) * 4 + ring
    right, left, far = lax.rem(ring + 1, 4), lax.rem(ring + 3, 4), lax.rem(ring + 2, 4)

    def copy(kind, ref, target):
        return pltpu.make_async_remote_copy(
            src_ref=ref,
            dst_ref=ref,
            send_sem=send.at[kind],
            recv_sem=recv.at[kind],
            device_id=device_of(target),
            device_id_type=MESH,
        )

    to_right, to_left = hi * 4 + right, hi * 4 + left
    from_left, from_right, across = hi * 4 + left, hi * 4 + right, hi * 4 + far
    mate_left, mate_right, mate_across = (1 - hi) * 4 + left, (1 - hi) * 4 + right, (1 - hi) * 4 + far

    if ring_first:
        relays = [(3, shard(from_left), mate), (4, shard(from_right), mate)]
        relays += [(5, piece(from_left, 0), to_right), (6, piece(from_right, 1), to_left)]
        relays += [(7, piece(across, 0), mate), (8, piece(across, 1), mate)]
    else:
        relays = [(3, shard(mate), to_right), (4, shard(mate), to_left)]
        relays += [(5, piece(from_left, 0), to_right), (6, piece(from_right, 1), to_left)]
        relays += [(7, piece(mate_left, 0), to_right), (8, piece(mate_right, 1), to_left)]
    sends = [
        (0, shard(own), mate),
        (1, shard(own), to_right),
        (2, shard(own), to_left),
    ] + relays
    landings = [
        shard(mate),
        shard(from_left),
        shard(from_right),
        shard(mate_left),
        shard(mate_right),
        piece(across, 0),
        piece(across, 1),
        piece(mate_across, 0),
        piece(mate_across, 1),
    ]

    def start(*kinds):
        for kind in kinds:
            copy(*sends[kind]).start()

    def arrived(*kinds):
        for kind in kinds:
            copy(kind, landings[kind], own).wait_recv()

    def begin():
        start(0, 1, 2)
        landed(own)

    def mid():
        if ring_first:
            arrived(1)
            start(5, 3)
            arrived(2)
            start(6, 4)
        else:
            arrived(0)
            start(3, 4)
            arrived(1)
            start(5)
            arrived(2)
            start(6)
        landed(mate)
        landed(from_left)
        landed(from_right)

    def late():
        if ring_first:
            arrived(5)
            start(7)
            arrived(6)
            start(8)
            return
        arrived(3)
        start(7)
        arrived(4)
        start(8)
        landed(mate_left)
        landed(mate_right)

    def finish():
        if ring_first:
            arrived(0, 3, 4, 7, 8)
            return
        arrived(5, 6, 7, 8)
        landed(across)
        landed(mate_across)

    def sent():
        for kind in range(KINDS):
            copy(*sends[kind]).wait_send()

    return begin, mid, late, finish, sent


def pair_kernel(
    weight, occ_in, emp_in, first, second, tw, out,
    occ, emp, z_hi, z_lo, high_0, low_0, high_1, low_1, local, o_send, o_recv, e_send, e_recv, s_send, s_recv,
):
    n_occ, n_emp = occ.shape[0], emp.shape[0]
    o = lax.axis_index("occ")
    m = lax.axis_index("emp")
    o_hi, o_ring = o // 4, lax.rem(o, 4)
    chip, core = m // 2, lax.rem(m, 2)
    c_hi, c_ring = chip // 4, lax.rem(chip, 4)

    def emp_band(c):
        return gather_steps(
            e_send.at[c], e_recv.at[c],
            lambda i: emp.at[c, :, i],
            lambda i, h: emp.at[c, h, i],
            o_hi, o_ring,
            lambda i: {"occ": i, "emp": m},
            ring_first=c in RING_FIRST,
        )

    def occ_band(v):
        return gather_steps(
            o_send.at[v], o_recv.at[v],
            lambda i: occ.at[v, core, i],
            lambda i, h: occ.at[v, core, i, h],
            c_hi, c_ring,
            lambda i: {"occ": o, "emp": 2 * i + core},
        )

    sibling = {"occ": o, "emp": 2 * chip + 1 - core}

    def share(v, mine):
        return pltpu.make_async_remote_copy(
            src_ref=occ.at[v, mine],
            dst_ref=occ.at[v, mine],
            send_sem=s_send.at[v],
            recv_sem=s_recv.at[v],
            device_id=sibling,
            device_id_type=MESH,
        )

    copies = []
    for v in range(n_occ):
        copies.append(pltpu.make_async_copy(occ_in.at[v], occ.at[v, core, chip], local.at[v]))
    for c in range(n_emp):
        copies.append(pltpu.make_async_copy(emp_in.at[c], emp.at[c, :, o], local.at[n_occ + c]))
    for copy in copies:
        copy.start()

    barrier = pltpu.get_barrier_semaphore()
    peers = [
        {"occ": (1 - o_hi) * 4 + o_ring, "emp": m},
        {"occ": o_hi * 4 + lax.rem(o_ring + 1, 4), "emp": m},
        {"occ": o_hi * 4 + lax.rem(o_ring + 3, 4), "emp": m},
        {"occ": o, "emp": 2 * ((1 - c_hi) * 4 + c_ring) + core},
        {"occ": o, "emp": 2 * (c_hi * 4 + lax.rem(c_ring + 1, 4)) + core},
        {"occ": o, "emp": 2 * (c_hi * 4 + lax.rem(c_ring + 3, 4)) + core},
        sibling,
    ]
    for peer in peers:
        pl.semaphore_signal(barrier, inc=1, device_id=peer, device_id_type=MESH)
    pl.semaphore_wait(barrier, len(peers))
    for copy in copies:
        copy.wait()

    E = [emp_band(c) for c in range(n_emp)]
    O = [occ_band(v) for v in range(n_occ)]

    def pass_on(v):
        O[v][FINISH]()
        share(v, core).start()

    def shared(v):
        share(v, 1 - core).wait_recv()

    for action in (
        E[0][BEGIN],
        O[0][BEGIN],
        O[1][BEGIN],
        O[2][BEGIN],
        O[3][BEGIN],
        E[1][BEGIN],
        E[0][MID],
        O[0][MID],
        O[1][MID],
        O[0][LATE],
        E[0][LATE],
        E[2][BEGIN],
        O[1][LATE],
        O[2][MID],
        lambda: pass_on(0),
        O[3][MID],
        O[2][LATE],
        E[0][FINISH],
        E[3][BEGIN],
        lambda: shared(0),
    ):
        action()

    steps = {
        1: (lambda: pass_on(1), E[1][MID], O[3][LATE],),
        4: (lambda: shared(1),),
        5: (E[1][LATE],),
        6: (lambda: pass_on(2),),
        7: (E[2][MID],),
        8: (lambda: shared(2),),
        11: (E[2][LATE],),
        12: (E[1][FINISH],),
        13: (E[3][MID],),
        14: (lambda: pass_on(3),),
        17: (E[3][LATE],),
        19: (lambda: shared(3),),
        32: (E[2][FINISH],),
        48: (E[3][FINISH],),
    }

    pairs = n_occ * n_emp
    highs, lows = (high_0, high_1), (low_0, low_1)

    def pair_at(n):
        late, extra = n // 8, n // 6
        early = 1 - late
        first_six = early * (1 - lax.rem(extra, 2))
        pair_of_last = early - first_six
        c = first_six * (n // 3) + pair_of_last * (n - 6) + late * (n // 4)
        v = first_six * lax.rem(n, 3) + pair_of_last * 3 + late * lax.rem(n, 4)
        return v, c

    def products(n, t):
        v, c = pair_at(n)
        high_to, low_to = highs[t % 2], lows[t % 2]
        for i in range(TILE):
            slab = t * TILE + i
            h, s = slab // 8, slab % 8
            rows = slice(i * ROWS, (i + 1) * ROWS)
            for q in range(3):
                vr = occ[v, h, s, 0, q].astype(f32)
                vi = occ[v, h, s, 1, q].astype(f32)
                cr = emp[c, h, s, 0, q].astype(f32)
                ci = emp[c, h, s, 1, q].astype(f32)
                for at, p in ((0, vr * cr + vi * ci), (1, vr * ci - vi * cr)):
                    lanes = slice((2 * q + at) * 128, (2 * q + at + 1) * 128)
                    high = p.astype(bf16)
                    high_to[rows, lanes] = high
                    low_to[rows, lanes] = (p - high.astype(f32)).astype(bf16)

    def transform_z(t):
        high, low = highs[t % 2], lows[t % 2]
        parts = []
        for q in range(3):
            table = first[q * 256 : (q + 1) * 256, :]
            chunk = slice(q * 256, (q + 1) * 256)
            both = jnp.dot(high[:, chunk], table, preferred_element_type=f32)
            more = jnp.dot(low[:, chunk], table[:, :128], preferred_element_type=f32)
            parts.append(both[:, :128] + (both[:, 128:] + more))
        upper = lax.broadcasted_iota(jnp.int32, parts[1].shape, 1) >= 64
        zero = jnp.zeros_like(parts[1])
        for at, z in (
            (0, parts[0] + jnp.where(upper, parts[1], zero)),
            (1, parts[2] + jnp.where(upper, zero, parts[1])),
        ):
            where = (slice(t * TILE * ROWS, (t + 1) * TILE * ROWS), slice(at * 128, (at + 1) * 128))
            high_z = z.astype(bf16)
            z_hi[where] = high_z
            z_lo[where] = (z - high_z.astype(f32)).astype(bf16)

    def swap(a):
        real = lax.rem(lax.broadcasted_iota(jnp.int32, a.shape, 1) // KZ, 2) == 0
        return jnp.where(real, pltpu.roll(a, a.shape[1] - KZ, 1), pltpu.roll(a, KZ, 1))

    def transform_xy(n):
        v, c = pair_at(n)
        big = jnp.dot(second[...], z_hi[...], preferred_element_type=f32)
        small = jnp.dot(second[: 2 * HALF, :], z_lo[...], preferred_element_type=f32)
        both = big[: 2 * HALF] + (big[2 * HALF :] + small)
        u = both[:HALF]
        real = lax.rem(lax.broadcasted_iota(jnp.int32, u.shape, 1) // KZ, 2) == 0
        w = swap(both[HALF:])
        w = jnp.where(real, w, -w)
        cos, sin = tw[0], tw[1]
        scale = weight[v, c]
        for sign in range(2):
            g = u + w if sign == 0 else u - w
            turned = sin * swap(g)
            full = (cos * g + turned if sign == 0 else cos * g - turned).T
            total = (full[: 2 * KZ] + full[2 * KZ : 4 * KZ]) + (full[4 * KZ : 6 * KZ] + full[6 * KZ :])
            total = (total * scale).astype(bf16).reshape(2, KZ, HALF)
            out[:, v, c, :, sign * HALF : (sign + 1) * HALF] = total

    products(0, 0)

    tiles = 16 // TILE

    def serve(n, t):
        for step, actions in steps.items():
            if step % tiles == t:

                @pl.when(n == step // tiles)
                def _(actions=actions):
                    for action in actions:
                        action()

    def one_pair(n, carry):
        for t in range(tiles):
            transform_z(t)
            if t + 1 < tiles:
                serve(n, t + 1)
                products(n, t + 1)
        serve(n + 1, 0)
        transform_xy(n)
        products(jnp.minimum(n + 1, pairs - 1), 0)
        return carry

    lax.fori_loop(0, pairs, one_pair, 0)
    for v in range(n_occ):
        O[v][SENT]()
        share(v, core).wait_send()
    for c in range(n_emp):
        E[c][SENT]()


TILE = 4


def compact(weight, occupied, empty):
    first, second, tw, unused = tables()
    n_occ, n_emp = occupied.shape[1], empty.shape[1]
    occ_in = occupied.reshape(2, n_occ, SLAB, GROUPS, 3, 128).transpose(1, 0, 4, 3, 2, 5)
    occ_in = occ_in.reshape(n_occ, 2, 3, ROWS, 128)
    emp_in = empty.reshape(2, n_emp, 2, SLAB, GROUPS, 3, 128).transpose(1, 2, 0, 5, 4, 3, 6)
    emp_in = emp_in.reshape(n_emp, 2, 2, 3, ROWS, 128)
    vmem = pl.BlockSpec(memory_space=pltpu.VMEM)
    hbm = pl.BlockSpec(memory_space=pl.ANY)
    dma = pltpu.SemaphoreType.DMA
    return pl.pallas_call(
        pair_kernel,
        out_shape=jax.ShapeDtypeStruct((2, n_occ, n_emp, KZ, 2 * HALF), bf16),
        in_specs=[pl.BlockSpec(memory_space=pltpu.SMEM), hbm, hbm] + [vmem] * 3,
        out_specs=vmem,
        scratch_shapes=[
            pltpu.VMEM((n_occ, 2, 8, 2, 3, ROWS, 128), bf16),
            pltpu.VMEM((n_emp, 2, 8, 2, 3, ROWS, 128), bf16),
            pltpu.VMEM((GROUPS * GRID, 256), bf16),
            pltpu.VMEM((GROUPS * GRID, 256), bf16),
            pltpu.VMEM((TILE * ROWS, 768), bf16),
            pltpu.VMEM((TILE * ROWS, 768), bf16),
            pltpu.VMEM((TILE * ROWS, 768), bf16),
            pltpu.VMEM((TILE * ROWS, 768), bf16),
            dma((n_occ + n_emp,)),
            dma((n_occ, KINDS)),
            dma((n_occ, KINDS)),
            dma((n_emp, KINDS)),
            dma((n_emp, KINDS)),
            dma((n_occ,)),
            dma((n_occ,)),
        ],
        compiler_params=pltpu.CompilerParams(
            vmem_limit_bytes=60 * 2**20, collective_id=0, has_side_effects=True
        ),
        name="pair_spectra",
    )(weight, occ_in, emp_in, first, second, tw)


def select_kernel(column, kxy, kz, x, out):
    hot = jnp.where(column[...] == kxy[0], 1.0, 0.0).astype(bf16)
    rows = x.shape[0] // KZ
    picked = jnp.dot(x[...], hot, preferred_element_type=f32)
    level = lax.broadcasted_iota(jnp.int32, (KZ, BLOCK_PAD), 0)
    mask = jnp.where(level == kz[0], 1.0, 0.0)
    total = jnp.sum(picked.reshape(rows, KZ, BLOCK_PAD) * mask[None], axis=1)
    out[0] = total.astype(bf16)


def select(gvec, x):
    column = tables()[3]
    blocks = NG // BLOCK
    padded = jnp.pad(gvec.reshape(blocks, 1, BLOCK), ((0, 0), (0, 0), (0, BLOCK_PAD - BLOCK)), constant_values=0)
    kxy = padded // KB
    kz = padded - kxy * KB
    live = lax.broadcasted_iota(jnp.int32, padded.shape, 2) < BLOCK
    kxy = jnp.where(live, kxy, -2)
    rows = x.shape[0] // KZ
    return pl.pallas_call(
        select_kernel,
        grid=(blocks,),
        out_shape=jax.ShapeDtypeStruct((blocks, rows, BLOCK_PAD), bf16),
        in_specs=[
            pl.BlockSpec((2 * HALF, 1), lambda b: (0, 0)),
            pl.BlockSpec((1, 1, BLOCK_PAD), lambda b: (b, 0, 0)),
            pl.BlockSpec((1, 1, BLOCK_PAD), lambda b: (b, 0, 0)),
            pl.BlockSpec(x.shape, lambda b: (0, 0)),
        ],
        out_specs=pl.BlockSpec((1, rows, BLOCK_PAD), lambda b: (b, 0, 0)),
        compiler_params=pltpu.CompilerParams(vmem_limit_bytes=40 * 2**20),
        name="sphere_select",
    )(column, kxy, kz, x)


def densities_of(occ_all, emp_all, occ_energy, emp_energy, gvec):
    weight = jnp.sqrt(4.0 / (emp_energy[None, :] - occ_energy[:, None])) / math.sqrt(GRID**3)
    x = compact(weight, occ_all, emp_all)
    rows = 2 * x.shape[1] * x.shape[2]
    return select(gvec, x.reshape(rows * KZ, 2 * HALF))


BEGIN, MID, LATE, FINISH, SENT = range(5)


def chi_kernel(factor, d, out, rows, cols, local, r_send, r_recv, c_send, c_recv, g_send, g_recv, s_send, s_recv):
    o = lax.axis_index("occ")
    m = lax.axis_index("emp")
    o_hi, o_ring = o // 4, lax.rem(o, 4)
    chip, core = m // 2, lax.rem(m, 2)
    c_hi, c_ring = chip // 4, lax.rem(chip, 4)

    def copy(src, dst, send, recv, device):
        return pltpu.make_async_remote_copy(
            src_ref=src, dst_ref=dst, send_sem=send, recv_sem=recv, device_id=device, device_id_type=MESH
        )

    own_copies = [pltpu.make_async_copy(d.at[2 * o + b], rows.at[b, core, o, chip], local.at[b]) for b in range(2)]
    own_copies.append(pltpu.make_async_copy(d.at[m], cols.at[core, o, chip], local.at[2]))
    for own_copy in own_copies:
        own_copy.start()

    barrier = pltpu.get_barrier_semaphore()
    for step in range(1, 8):
        peer = {"occ": lax.rem(o + step, 8), "emp": m}
        pl.semaphore_signal(barrier, inc=1, device_id=peer, device_id_type=MESH)
    for step in range(1, 16):
        peer = {"occ": o, "emp": lax.rem(m + step, 16)}
        pl.semaphore_signal(barrier, inc=1, device_id=peer, device_id_type=MESH)
    pl.semaphore_wait(barrier, 22)

    def row_part(b, step):
        to = lax.rem(o + step, 8)
        return copy(
            d.at[2 * to + b], rows.at[b, core, o, chip], r_send.at[b, step - 1], r_recv.at[b, step - 1],
            {"occ": to, "emp": m},
        )

    def row_landing(b, step):
        here = rows.at[b, core, lax.rem(o + 8 - step, 8), chip]
        return copy(here, here, r_send.at[b, step - 1], r_recv.at[b, step - 1], {"occ": o, "emp": m})

    def col_part(step):
        to = lax.rem(m + step, 16)
        return copy(
            d.at[to], cols.at[core, o, chip], c_send.at[step - 1], c_recv.at[step - 1], {"occ": o, "emp": to}
        )

    def col_landing(step):
        source = lax.rem(m + 16 - step, 16)
        here = cols.at[lax.rem(source, 2), o, source // 2]
        return copy(here, here, c_send.at[step - 1], c_recv.at[step - 1], {"occ": o, "emp": m})

    row_steps = range(1, 8)
    even, odd = range(2, 16, 2), range(1, 16, 2)
    for step in row_steps:
        row_part(0, step).start()
    for step in even:
        col_part(step).start()
    for step in row_steps:
        row_part(1, step).start()
    for step in odd:
        col_part(step).start()

    sibling = {"occ": o, "emp": 2 * chip + 1 - core}

    def share(b, mine, i):
        here = rows.at[b, mine, :, i]
        return copy(here, here, s_send.at[b, i], s_recv.at[b, i], sibling)

    def row_band(b):
        return gather_steps(
            g_send.at[b], g_recv.at[b],
            lambda i: rows.at[b, core, :, i],
            lambda i, h: rows.at[b, core, pl.ds(4 * h, 4), i],
            c_hi, c_ring,
            lambda i: {"occ": o, "emp": 2 * i + core},
            lambda i: share(b, core, i).start(),
        )

    def col_band(j):
        k = core if j == 0 else 1 - core
        return gather_steps(
            g_send.at[2 + j], g_recv.at[2 + j],
            lambda i: cols.at[k, i],
            lambda i, h: cols.at[k, i, pl.ds(4 * h, 4)],
            o_hi, o_ring,
            lambda i: {"occ": i, "emp": m},
        )

    R = [row_band(b) for b in range(2)]
    C = [col_band(j) for j in range(2)]
    for own_copy in own_copies:
        own_copy.wait()
    for step in row_steps:
        row_landing(0, step).wait_recv()
    R[0][BEGIN]()
    for step in even:
        col_landing(step).wait_recv()
    C[0][BEGIN]()
    for step in row_steps:
        row_landing(1, step).wait_recv()
    R[1][BEGIN]()
    for step in odd:
        col_landing(step).wait_recv()
    C[1][BEGIN]()
    for part in (MID, LATE, FINISH):
        for band in (R[0], C[0], R[1], C[1]):
            band[part]()

    depth = rows.shape[2] * rows.shape[3] * rows.shape[4]
    half = rows.shape[4] // 2

    def multiply(k, last):
        right = cols[k].reshape(depth // (2 * half), 2 * half, BLOCK_PAD)
        turned = jnp.concatenate([-right[:, half:], right[:, :half]], axis=1)
        right = right.reshape(depth, BLOCK_PAD)
        turned = turned.reshape(depth, BLOCK_PAD)
        for b in range(2):
            left = rows[b, k].reshape(depth, BLOCK_PAD)
            for at, side in ((0, right), (1, turned)):
                part = lax.dot_general(left, side, (((0,), (0,)), ((), ())), preferred_element_type=f32)
                out[at, b] = (out[at, b] + part) * factor if last else part

    multiply(core, False)
    for b in range(2):
        for i in range(8):
            share(b, 1 - core, i).wait_recv()
    multiply(1 - core, True)
    for step in row_steps:
        for b in range(2):
            row_part(b, step).wait_send()
    for step in range(1, 16):
        col_part(step).wait_send()
    for band in R + C:
        band[SENT]()
    for b in range(2):
        for i in range(8):
            share(b, core, i).wait_send()


def body(occupied, empty, occ_energy, emp_energy, gvec):
    d = densities_of(occupied, empty, occ_energy, emp_energy, gvec)
    rows = d.shape[1]
    n_occ = lax.axis_size("occ")
    n_emp = lax.axis_size("emp")
    factor = -1.0 / math.sqrt(n_occ * n_emp * (rows // 2))
    vmem = pl.BlockSpec(memory_space=pltpu.VMEM)
    dma = pltpu.SemaphoreType.DMA
    chi = pl.pallas_call(
        functools.partial(chi_kernel, factor),
        out_shape=jax.ShapeDtypeStruct((2, 2, BLOCK_PAD, BLOCK_PAD), f32),
        in_specs=[pl.BlockSpec(memory_space=pl.ANY)],
        out_specs=vmem,
        scratch_shapes=[
            pltpu.VMEM((2, 2, 8, 8, rows, BLOCK_PAD), bf16),
            pltpu.VMEM((2, 8, 8, rows, BLOCK_PAD), bf16),
            dma((3,)),
            dma((2, 7)),
            dma((2, 7)),
            dma((15,)),
            dma((15,)),
            dma((4, KINDS)),
            dma((4, KINDS)),
            dma((2, 8)),
            dma((2, 8)),
        ],
        compiler_params=pltpu.CompilerParams(
            vmem_limit_bytes=56 * 2**20, collective_id=1, has_side_effects=True
        ),
        name="chi_blocks",
    )(d)
    return chi[:, :, :BLOCK, :BLOCK].reshape(2, 2 * BLOCK, BLOCK)


def solution(mesh):
    placed = (P(None, "occ", "emp", None), P(None, "emp", "occ", None), P("occ"), P("emp"), P())
    return jax.shard_map(
        body, mesh=mesh, in_specs=placed, out_specs=P(None, "occ", "emp"), check_vma=False
    )
```

```python
import functools
import math

import jax
import jax.numpy as jnp
import ml_dtypes
import numpy as np
from jax import lax
from jax.experimental import pallas as pl
from jax.experimental.pallas import tpu as pltpu
from jax.sharding import PartitionSpec as P

GRID = 96
KB = 25
REACH = KB // 2
NG = 8000
RSQ = 153
GROUPS = 24
SLAB = 6
ROWS = GROUPS * SLAB
HALF = 256
KZ = 32
CHUNK_Y = ((0, 1), (2, 1), (2, 3))
RING_FIRST = ()
BLOCK = 500
BLOCK_PAD = 512

f32 = jnp.float32
bf16 = jnp.bfloat16


def split(table):
    high = table.astype(ml_dtypes.bfloat16)
    low = (table - high.astype(np.float64)).astype(ml_dtypes.bfloat16)
    return high, low


def half_disc():
    kept = []
    for kx in range(-REACH, REACH + 1):
        for ky in range(-REACH, REACH + 1):
            if kx * kx + ky * ky <= RSQ and (kx > 0 or (kx == 0 and ky >= 0)):
                kept.append((kx, ky))
    return np.array(kept)


def tables():
    theta = 2.0 * np.pi / GRID
    disc = half_disc()
    kx, ky = disc[:, 0], disc[:, 1]
    freq = (np.arange(KB) + REACH) % KB - REACH
    first = np.zeros((3, 2, 128, 2, 2, KZ))
    for q in range(3):
        for lane in range(128):
            y, z = divmod(q * 128 + lane, GRID)
            slot = CHUNK_Y[q].index(y)
            angle = theta * (z * freq % GRID)
            first[q, 0, lane, slot, 0, :KB] = np.cos(angle)
            first[q, 0, lane, slot, 1, :KB] = -np.sin(angle)
            first[q, 1, lane, slot, 0, :KB] = np.sin(angle)
            first[q, 1, lane, slot, 1, :KB] = np.cos(angle)
    first = first.reshape(768, 128)
    half, slab, j, x = [a.reshape(-1) for a in np.meshgrid(*map(np.arange, (2, 8, GROUPS, SLAB)), indexing="ij")]
    x = 2 * SLAB * slab + SLAB * half + x
    angle = theta * ((np.outer(kx, x) + 4 * np.outer(ky, j)) % GRID)
    second = np.zeros((2, HALF, GROUPS * GRID))
    second[0, : len(disc)] = np.cos(angle)
    second[1, : len(disc)] = np.sin(angle)
    second = second.reshape(2 * HALF, GROUPS * GRID)
    angle = theta * ((ky[:, None] * np.repeat(np.arange(4), 2 * KZ)[None, :]) % GRID)
    turn = np.tile(np.repeat([1.0, -1.0], KZ), 4)
    twiddle = np.zeros((2, HALF, 8 * KZ), np.float32)
    twiddle[0, : len(disc)] = np.cos(angle)
    twiddle[1, : len(disc)] = np.sin(angle) * turn
    column = np.full((2, HALF), -1, np.int32)
    column[0, : len(disc)] = (kx % KB) * KB + ky % KB
    column[1, 1 : len(disc)] = ((-kx) % KB)[1:] * KB + ((-ky) % KB)[1:]
    first_hi, first_lo = split(first)
    first = np.concatenate([first_hi, first_lo], axis=1)
    second = np.concatenate(split(second), axis=0)
    return first, second, twiddle, column.reshape(2 * HALF, 1)


MESH = pl.DeviceIdType.MESH
KINDS = 9


def gather_steps(send, recv, shard, piece, hi, ring, device_of, landed=lambda i: None, ring_first=False):
    own = hi * 4 + ring
    mate = (1 - hi) * 4 + ring
    right, left, far = lax.rem(ring + 1, 4), lax.rem(ring + 3, 4), lax.rem(ring + 2, 4)

    def copy(kind, ref, target):
        return pltpu.make_async_remote_copy(
            src_ref=ref,
            dst_ref=ref,
            send_sem=send.at[kind],
            recv_sem=recv.at[kind],
            device_id=device_of(target),
            device_id_type=MESH,
        )

    to_right, to_left = hi * 4 + right, hi * 4 + left
    from_left, from_right, across = hi * 4 + left, hi * 4 + right, hi * 4 + far
    mate_left, mate_right, mate_across = (1 - hi) * 4 + left, (1 - hi) * 4 + right, (1 - hi) * 4 + far

    if ring_first:
        relays = [(3, shard(from_left), mate), (4, shard(from_right), mate)]
        relays += [(5, piece(from_left, 0), to_right), (6, piece(from_right, 1), to_left)]
        relays += [(7, piece(across, 0), mate), (8, piece(across, 1), mate)]
    else:
        relays = [(3, shard(mate), to_right), (4, shard(mate), to_left)]
        relays += [(5, piece(from_left, 0), to_right), (6, piece(from_right, 1), to_left)]
        relays += [(7, piece(mate_left, 0), to_right), (8, piece(mate_right, 1), to_left)]
    sends = [
        (0, shard(own), mate),
        (1, shard(own), to_right),
        (2, shard(own), to_left),
    ] + relays
    landings = [
        shard(mate),
        shard(from_left),
        shard(from_right),
        shard(mate_left),
        shard(mate_right),
        piece(across, 0),
        piece(across, 1),
        piece(mate_across, 0),
        piece(mate_across, 1),
    ]

    def start(*kinds):
        for kind in kinds:
            copy(*sends[kind]).start()

    def arrived(*kinds):
        for kind in kinds:
            copy(kind, landings[kind], own).wait_recv()

    def begin():
        start(0, 1, 2)
        landed(own)

    def mid():
        if ring_first:
            arrived(1)
            start(5, 3)
            arrived(2)
            start(6, 4)
        else:
            arrived(0)
            start(3, 4)
            arrived(1)
            start(5)
            arrived(2)
            start(6)
        landed(mate)
        landed(from_left)
        landed(from_right)

    def late():
        if ring_first:
            arrived(5)
            start(7)
            arrived(6)
            start(8)
            return
        arrived(3)
        start(7)
        arrived(4)
        start(8)
        landed(mate_left)
        landed(mate_right)

    def finish():
        if ring_first:
            arrived(0, 3, 4, 7, 8)
            return
        arrived(5, 6, 7, 8)
        landed(across)
        landed(mate_across)

    def sent():
        for kind in range(KINDS):
            copy(*sends[kind]).wait_send()

    return begin, mid, late, finish, sent


def pair_kernel(
    weight, occ_in, emp_in, first, second, tw, out,
    occ, emp, z_hi, z_lo, high_0, low_0, high_1, low_1, local, o_send, o_recv, e_send, e_recv, s_send, s_recv,
):
    n_occ, n_emp = occ.shape[0], emp.shape[0]
    o = lax.axis_index("occ")
    m = lax.axis_index("emp")
    o_hi, o_ring = o // 4, lax.rem(o, 4)
    chip, core = m // 2, lax.rem(m, 2)
    c_hi, c_ring = chip // 4, lax.rem(chip, 4)

    def emp_band(c):
        return gather_steps(
            e_send.at[c], e_recv.at[c],
            lambda i: emp.at[c, :, i],
            lambda i, h: emp.at[c, h, i],
            o_hi, o_ring,
            lambda i: {"occ": i, "emp": m},
            ring_first=c in RING_FIRST,
        )

    def occ_band(v):
        return gather_steps(
            o_send.at[v], o_recv.at[v],
            lambda i: occ.at[v, core, i],
            lambda i, h: occ.at[v, core, i, h],
            c_hi, c_ring,
            lambda i: {"occ": o, "emp": 2 * i + core},
        )

    sibling = {"occ": o, "emp": 2 * chip + 1 - core}

    def share(v, mine):
        return pltpu.make_async_remote_copy(
            src_ref=occ.at[v, mine],
            dst_ref=occ.at[v, mine],
            send_sem=s_send.at[v],
            recv_sem=s_recv.at[v],
            device_id=sibling,
            device_id_type=MESH,
        )

    copies = []
    for v in range(n_occ):
        copies.append(pltpu.make_async_copy(occ_in.at[v], occ.at[v, core, chip], local.at[v]))
    for c in range(n_emp):
        copies.append(pltpu.make_async_copy(emp_in.at[c], emp.at[c, :, o], local.at[n_occ + c]))
    for copy in copies:
        copy.start()

    barrier = pltpu.get_barrier_semaphore()
    peers = [
        {"occ": (1 - o_hi) * 4 + o_ring, "emp": m},
        {"occ": o_hi * 4 + lax.rem(o_ring + 1, 4), "emp": m},
        {"occ": o_hi * 4 + lax.rem(o_ring + 3, 4), "emp": m},
        {"occ": o, "emp": 2 * ((1 - c_hi) * 4 + c_ring) + core},
        {"occ": o, "emp": 2 * (c_hi * 4 + lax.rem(c_ring + 1, 4)) + core},
        {"occ": o, "emp": 2 * (c_hi * 4 + lax.rem(c_ring + 3, 4)) + core},
        sibling,
    ]
    for peer in peers:
        pl.semaphore_signal(barrier, inc=1, device_id=peer, device_id_type=MESH)
    pl.semaphore_wait(barrier, len(peers))
    for copy in copies:
        copy.wait()

    E = [emp_band(c) for c in range(n_emp)]
    O = [occ_band(v) for v in range(n_occ)]

    def pass_on(v):
        O[v][FINISH]()
        share(v, core).start()

    def shared(v):
        share(v, 1 - core).wait_recv()

    for action in (
        E[0][BEGIN],
        O[0][BEGIN],
        O[1][BEGIN],
        O[0][MID],
        E[0][MID],
        O[0][LATE],
        O[2][BEGIN],
        lambda: pass_on(0),
        E[0][LATE],
        E[1][BEGIN],
        O[1][MID],
        O[1][LATE],
        O[3][BEGIN],
        E[0][FINISH],
        lambda: shared(0),
    ):
        action()

    steps = {
        2: (lambda: pass_on(1),),
        3: (E[1][MID], E[2][BEGIN],),
        4: (lambda: shared(1), O[2][MID],),
        6: (E[1][LATE],),
        7: (O[2][LATE],),
        8: (lambda: pass_on(2), lambda: shared(2),),
        10: (O[3][MID],),
        12: (E[1][FINISH], E[2][MID], E[3][BEGIN],),
        13: (O[3][LATE],),
        15: (lambda: pass_on(3),),
        17: (E[2][LATE],),
        18: (lambda: shared(3),),
        23: (E[3][MID],),
        28: (E[3][LATE],),
        32: (E[2][FINISH],),
        48: (E[3][FINISH],),
    }

    pairs = n_occ * n_emp
    highs, lows = (high_0, high_1), (low_0, low_1)

    def pair_at(n):
        late, extra = n // 8, n // 6
        early = 1 - late
        first_six = early * (1 - lax.rem(extra, 2))
        pair_of_last = early - first_six
        c = first_six * (n // 3) + pair_of_last * (n - 6) + late * (n // 4)
        v = first_six * lax.rem(n, 3) + pair_of_last * 3 + late * lax.rem(n, 4)
        return v, c

    def products(n, t):
        v, c = pair_at(n)
        high_to, low_to = highs[t % 2], lows[t % 2]
        for i in range(TILE):
            slab = t * TILE + i
            h, s = slab // 8, slab % 8
            rows = slice(i * ROWS, (i + 1) * ROWS)
            for q in range(3):
                vr = occ[v, h, s, 0, q].astype(f32)
                vi = occ[v, h, s, 1, q].astype(f32)
                cr = emp[c, h, s, 0, q].astype(f32)
                ci = emp[c, h, s, 1, q].astype(f32)
                for at, p in ((0, vr * cr + vi * ci), (1, vr * ci - vi * cr)):
                    lanes = slice((2 * q + at) * 128, (2 * q + at + 1) * 128)
                    high = p.astype(bf16)
                    high_to[rows, lanes] = high
                    low_to[rows, lanes] = (p - high.astype(f32)).astype(bf16)

    def transform_z(t):
        high, low = highs[t % 2], lows[t % 2]
        parts = []
        for q in range(3):
            table = first[q * 256 : (q + 1) * 256, :]
            chunk = slice(q * 256, (q + 1) * 256)
            both = jnp.dot(high[:, chunk], table, preferred_element_type=f32)
            more = jnp.dot(low[:, chunk], table[:, :128], preferred_element_type=f32)
            parts.append(both[:, :128] + (both[:, 128:] + more))
        upper = lax.broadcasted_iota(jnp.int32, parts[1].shape, 1) >= 64
        zero = jnp.zeros_like(parts[1])
        for at, z in (
            (0, parts[0] + jnp.where(upper, parts[1], zero)),
            (1, parts[2] + jnp.where(upper, zero, parts[1])),
        ):
            where = (slice(t * TILE * ROWS, (t + 1) * TILE * ROWS), slice(at * 128, (at + 1) * 128))
            high_z = z.astype(bf16)
            z_hi[where] = high_z
            z_lo[where] = (z - high_z.astype(f32)).astype(bf16)

    def swap(a):
        real = lax.rem(lax.broadcasted_iota(jnp.int32, a.shape, 1) // KZ, 2) == 0
        return jnp.where(real, pltpu.roll(a, a.shape[1] - KZ, 1), pltpu.roll(a, KZ, 1))

    def transform_xy(n):
        v, c = pair_at(n)
        big = jnp.dot(second[...], z_hi[...], preferred_element_type=f32)
        small = jnp.dot(second[: 2 * HALF, :], z_lo[...], preferred_element_type=f32)
        both = big[: 2 * HALF] + (big[2 * HALF :] + small)
        u = both[:HALF]
        real = lax.rem(lax.broadcasted_iota(jnp.int32, u.shape, 1) // KZ, 2) == 0
        w = swap(both[HALF:])
        w = jnp.where(real, w, -w)
        cos, sin = tw[0], tw[1]
        scale = weight[v, c]
        for sign in range(2):
            g = u + w if sign == 0 else u - w
            turned = sin * swap(g)
            full = (cos * g + turned if sign == 0 else cos * g - turned).T
            total = (full[: 2 * KZ] + full[2 * KZ : 4 * KZ]) + (full[4 * KZ : 6 * KZ] + full[6 * KZ :])
            total = (total * scale).astype(bf16).reshape(2, KZ, HALF)
            out[:, v, c, :, sign * HALF : (sign + 1) * HALF] = total

    products(0, 0)

    tiles = 16 // TILE

    def serve(n, t):
        for step, actions in steps.items():
            if step % tiles == t:

                @pl.when(n == step // tiles)
                def _(actions=actions):
                    for action in actions:
                        action()

    def one_pair(n, carry):
        for t in range(tiles):
            transform_z(t)
            if t + 1 < tiles:
                serve(n, t + 1)
                products(n, t + 1)
        serve(n + 1, 0)
        transform_xy(n)
        products(jnp.minimum(n + 1, pairs - 1), 0)
        return carry

    lax.fori_loop(0, pairs, one_pair, 0)
    for v in range(n_occ):
        O[v][SENT]()
        share(v, core).wait_send()
    for c in range(n_emp):
        E[c][SENT]()


TILE = 4


def compact(weight, occupied, empty):
    first, second, tw, unused = tables()
    n_occ, n_emp = occupied.shape[1], empty.shape[1]
    occ_in = occupied.reshape(2, n_occ, SLAB, GROUPS, 3, 128).transpose(1, 0, 4, 3, 2, 5)
    occ_in = occ_in.reshape(n_occ, 2, 3, ROWS, 128)
    emp_in = empty.reshape(2, n_emp, 2, SLAB, GROUPS, 3, 128).transpose(1, 2, 0, 5, 4, 3, 6)
    emp_in = emp_in.reshape(n_emp, 2, 2, 3, ROWS, 128)
    vmem = pl.BlockSpec(memory_space=pltpu.VMEM)
    hbm = pl.BlockSpec(memory_space=pl.ANY)
    dma = pltpu.SemaphoreType.DMA
    return pl.pallas_call(
        pair_kernel,
        out_shape=jax.ShapeDtypeStruct((2, n_occ, n_emp, KZ, 2 * HALF), bf16),
        in_specs=[pl.BlockSpec(memory_space=pltpu.SMEM), hbm, hbm] + [vmem] * 3,
        out_specs=vmem,
        scratch_shapes=[
            pltpu.VMEM((n_occ, 2, 8, 2, 3, ROWS, 128), bf16),
            pltpu.VMEM((n_emp, 2, 8, 2, 3, ROWS, 128), bf16),
            pltpu.VMEM((GROUPS * GRID, 256), bf16),
            pltpu.VMEM((GROUPS * GRID, 256), bf16),
            pltpu.VMEM((TILE * ROWS, 768), bf16),
            pltpu.VMEM((TILE * ROWS, 768), bf16),
            pltpu.VMEM((TILE * ROWS, 768), bf16),
            pltpu.VMEM((TILE * ROWS, 768), bf16),
            dma((n_occ + n_emp,)),
            dma((n_occ, KINDS)),
            dma((n_occ, KINDS)),
            dma((n_emp, KINDS)),
            dma((n_emp, KINDS)),
            dma((n_occ,)),
            dma((n_occ,)),
        ],
        compiler_params=pltpu.CompilerParams(
            vmem_limit_bytes=60 * 2**20, collective_id=0, has_side_effects=True
        ),
        name="pair_spectra",
    )(weight, occ_in, emp_in, first, second, tw)


def select_kernel(column, kxy, kz, x, out):
    hot = jnp.where(column[...] == kxy[0], 1.0, 0.0).astype(bf16)
    rows = x.shape[0] // KZ
    picked = jnp.dot(x[...], hot, preferred_element_type=f32)
    level = lax.broadcasted_iota(jnp.int32, (KZ, BLOCK_PAD), 0)
    mask = jnp.where(level == kz[0], 1.0, 0.0)
    total = jnp.sum(picked.reshape(rows, KZ, BLOCK_PAD) * mask[None], axis=1)
    out[0] = total.astype(bf16)


def select(gvec, x):
    column = tables()[3]
    blocks = NG // BLOCK
    padded = jnp.pad(gvec.reshape(blocks, 1, BLOCK), ((0, 0), (0, 0), (0, BLOCK_PAD - BLOCK)), constant_values=0)
    kxy = padded // KB
    kz = padded - kxy * KB
    live = lax.broadcasted_iota(jnp.int32, padded.shape, 2) < BLOCK
    kxy = jnp.where(live, kxy, -2)
    rows = x.shape[0] // KZ
    return pl.pallas_call(
        select_kernel,
        grid=(blocks,),
        out_shape=jax.ShapeDtypeStruct((blocks, rows, BLOCK_PAD), bf16),
        in_specs=[
            pl.BlockSpec((2 * HALF, 1), lambda b: (0, 0)),
            pl.BlockSpec((1, 1, BLOCK_PAD), lambda b: (b, 0, 0)),
            pl.BlockSpec((1, 1, BLOCK_PAD), lambda b: (b, 0, 0)),
            pl.BlockSpec(x.shape, lambda b: (0, 0)),
        ],
        out_specs=pl.BlockSpec((1, rows, BLOCK_PAD), lambda b: (b, 0, 0)),
        compiler_params=pltpu.CompilerParams(vmem_limit_bytes=40 * 2**20),
        name="sphere_select",
    )(column, kxy, kz, x)


def densities_of(occ_all, emp_all, occ_energy, emp_energy, gvec):
    weight = jnp.sqrt(4.0 / (emp_energy[None, :] - occ_energy[:, None])) / math.sqrt(GRID**3)
    x = compact(weight, occ_all, emp_all)
    rows = 2 * x.shape[1] * x.shape[2]
    return select(gvec, x.reshape(rows * KZ, 2 * HALF))


BEGIN, MID, LATE, FINISH, SENT = range(5)


def chi_kernel(factor, d, out, rows, cols, local, r_send, r_recv, c_send, c_recv, g_send, g_recv, s_send, s_recv):
    o = lax.axis_index("occ")
    m = lax.axis_index("emp")
    o_hi, o_ring = o // 4, lax.rem(o, 4)
    chip, core = m // 2, lax.rem(m, 2)
    c_hi, c_ring = chip // 4, lax.rem(chip, 4)

    def copy(src, dst, send, recv, device):
        return pltpu.make_async_remote_copy(
            src_ref=src, dst_ref=dst, send_sem=send, recv_sem=recv, device_id=device, device_id_type=MESH
        )

    own_copies = [pltpu.make_async_copy(d.at[2 * o + b], rows.at[b, core, o, chip], local.at[b]) for b in range(2)]
    own_copies.append(pltpu.make_async_copy(d.at[m], cols.at[core, o, chip], local.at[2]))
    for own_copy in own_copies:
        own_copy.start()

    barrier = pltpu.get_barrier_semaphore()
    for step in range(1, 8):
        peer = {"occ": lax.rem(o + step, 8), "emp": m}
        pl.semaphore_signal(barrier, inc=1, device_id=peer, device_id_type=MESH)
    for step in range(1, 16):
        peer = {"occ": o, "emp": lax.rem(m + step, 16)}
        pl.semaphore_signal(barrier, inc=1, device_id=peer, device_id_type=MESH)
    pl.semaphore_wait(barrier, 22)

    def row_part(b, step):
        to = lax.rem(o + step, 8)
        return copy(
            d.at[2 * to + b], rows.at[b, core, o, chip], r_send.at[b, step - 1], r_recv.at[b, step - 1],
            {"occ": to, "emp": m},
        )

    def row_landing(b, step):
        here = rows.at[b, core, lax.rem(o + 8 - step, 8), chip]
        return copy(here, here, r_send.at[b, step - 1], r_recv.at[b, step - 1], {"occ": o, "emp": m})

    def col_part(step):
        to = lax.rem(m + step, 16)
        return copy(
            d.at[to], cols.at[core, o, chip], c_send.at[step - 1], c_recv.at[step - 1], {"occ": o, "emp": to}
        )

    def col_landing(step):
        source = lax.rem(m + 16 - step, 16)
        here = cols.at[lax.rem(source, 2), o, source // 2]
        return copy(here, here, c_send.at[step - 1], c_recv.at[step - 1], {"occ": o, "emp": m})

    row_steps = range(1, 8)
    even, odd = range(2, 16, 2), range(1, 16, 2)
    for step in row_steps:
        row_part(0, step).start()
    for step in even:
        col_part(step).start()
    for step in row_steps:
        row_part(1, step).start()
    for step in odd:
        col_part(step).start()

    sibling = {"occ": o, "emp": 2 * chip + 1 - core}

    def share(b, mine, i):
        here = rows.at[b, mine, :, i]
        return copy(here, here, s_send.at[b, i], s_recv.at[b, i], sibling)

    def row_band(b):
        return gather_steps(
            g_send.at[b], g_recv.at[b],
            lambda i: rows.at[b, core, :, i],
            lambda i, h: rows.at[b, core, pl.ds(4 * h, 4), i],
            c_hi, c_ring,
            lambda i: {"occ": o, "emp": 2 * i + core},
            lambda i: share(b, core, i).start(),
        )

    def col_band(j):
        k = core if j == 0 else 1 - core
        return gather_steps(
            g_send.at[2 + j], g_recv.at[2 + j],
            lambda i: cols.at[k, i],
            lambda i, h: cols.at[k, i, pl.ds(4 * h, 4)],
            o_hi, o_ring,
            lambda i: {"occ": i, "emp": m},
        )

    R = [row_band(b) for b in range(2)]
    C = [col_band(j) for j in range(2)]
    for own_copy in own_copies:
        own_copy.wait()
    for step in row_steps:
        row_landing(0, step).wait_recv()
    R[0][BEGIN]()
    for step in even:
        col_landing(step).wait_recv()
    C[0][BEGIN]()
    for step in row_steps:
        row_landing(1, step).wait_recv()
    R[1][BEGIN]()
    for step in odd:
        col_landing(step).wait_recv()
    C[1][BEGIN]()
    for part in (MID, LATE):
        for band in (R[0], C[0], R[1], C[1]):
            band[part]()
    R[0][FINISH]()
    C[0][FINISH]()
    R[1][FINISH]()

    depth = rows.shape[2] * rows.shape[3] * rows.shape[4]
    half = rows.shape[4] // 2

    def multiply(k, blocks, last):
        right = cols[k].reshape(depth // (2 * half), 2 * half, BLOCK_PAD)
        turned = jnp.concatenate([-right[:, half:], right[:, :half]], axis=1)
        right = right.reshape(depth, BLOCK_PAD)
        turned = turned.reshape(depth, BLOCK_PAD)
        for b in blocks:
            left = rows[b, k].reshape(depth, BLOCK_PAD)
            for at, side in ((0, right), (1, turned)):
                part = lax.dot_general(left, side, (((0,), (0,)), ((), ())), preferred_element_type=f32)
                part = part[:BLOCK, :BLOCK]
                out[at, b] = (out[at, b] + part) * factor if last else part

    multiply(core, (0, 1), False)
    C[1][FINISH]()
    for b in range(2):
        for i in range(8):
            share(b, 1 - core, i).wait_recv()
    multiply(1 - core, (0, 1), True)
    for step in row_steps:
        for b in range(2):
            row_part(b, step).wait_send()
    for step in range(1, 16):
        col_part(step).wait_send()
    for band in R + C:
        band[SENT]()
    for b in range(2):
        for i in range(8):
            share(b, core, i).wait_send()


def body(occupied, empty, occ_energy, emp_energy, gvec):
    d = densities_of(occupied, empty, occ_energy, emp_energy, gvec)
    rows = d.shape[1]
    n_occ = lax.axis_size("occ")
    n_emp = lax.axis_size("emp")
    factor = -1.0 / math.sqrt(n_occ * n_emp * (rows // 2))
    vmem = pl.BlockSpec(memory_space=pltpu.VMEM)
    dma = pltpu.SemaphoreType.DMA
    chi = pl.pallas_call(
        functools.partial(chi_kernel, factor),
        out_shape=jax.ShapeDtypeStruct((2, 2, BLOCK, BLOCK), f32),
        in_specs=[pl.BlockSpec(memory_space=pl.ANY)],
        out_specs=vmem,
        scratch_shapes=[
            pltpu.VMEM((2, 2, 8, 8, rows, BLOCK_PAD), bf16),
            pltpu.VMEM((2, 8, 8, rows, BLOCK_PAD), bf16),
            dma((3,)),
            dma((2, 7)),
            dma((2, 7)),
            dma((15,)),
            dma((15,)),
            dma((4, KINDS)),
            dma((4, KINDS)),
            dma((2, 8)),
            dma((2, 8)),
        ],
        compiler_params=pltpu.CompilerParams(
            vmem_limit_bytes=56 * 2**20, collective_id=1, has_side_effects=True
        ),
        name="chi_blocks",
    )(d)
    return chi.reshape(2, 2 * BLOCK, BLOCK)


def solution(mesh):
    placed = (P(None, "occ", "emp", None), P(None, "emp", "occ", None), P("occ"), P("emp"), P())
    return jax.shard_map(
        body, mesh=mesh, in_specs=placed, out_specs=P(None, "occ", "emp"), check_vma=False
    )
```

```python
import functools
import math

import jax
import jax.numpy as jnp
import ml_dtypes
import numpy as np
from jax import lax
from jax.experimental import pallas as pl
from jax.experimental.pallas import tpu as pltpu
from jax.sharding import PartitionSpec as P

GRID = 96
KB = 25
REACH = KB // 2
NG = 8000
RSQ = 153
GROUPS = 24
SLAB = 6
ROWS = GROUPS * SLAB
HALF = 256
KZ = 32
CHUNK_Y = ((0, 1), (2, 1), (2, 3))
RING_FIRST = (3,)
BLOCK = 500
BLOCK_PAD = 512

f32 = jnp.float32
bf16 = jnp.bfloat16


def split(table):
    high = table.astype(ml_dtypes.bfloat16)
    low = (table - high.astype(np.float64)).astype(ml_dtypes.bfloat16)
    return high, low


def half_disc():
    kept = []
    for kx in range(-REACH, REACH + 1):
        for ky in range(-REACH, REACH + 1):
            if kx * kx + ky * ky <= RSQ and (kx > 0 or (kx == 0 and ky >= 0)):
                kept.append((kx, ky))
    return np.array(kept)


def tables():
    theta = 2.0 * np.pi / GRID
    disc = half_disc()
    kx, ky = disc[:, 0], disc[:, 1]
    freq = (np.arange(KB) + REACH) % KB - REACH
    first = np.zeros((3, 2, 128, 2, 2, KZ))
    for q in range(3):
        for lane in range(128):
            y, z = divmod(q * 128 + lane, GRID)
            slot = CHUNK_Y[q].index(y)
            angle = theta * (z * freq % GRID)
            first[q, 0, lane, slot, 0, :KB] = np.cos(angle)
            first[q, 0, lane, slot, 1, :KB] = -np.sin(angle)
            first[q, 1, lane, slot, 0, :KB] = np.sin(angle)
            first[q, 1, lane, slot, 1, :KB] = np.cos(angle)
    first = first.reshape(768, 128)
    half, slab, j, x = [a.reshape(-1) for a in np.meshgrid(*map(np.arange, (2, 8, GROUPS, SLAB)), indexing="ij")]
    x = 2 * SLAB * slab + SLAB * half + x
    angle = theta * ((np.outer(kx, x) + 4 * np.outer(ky, j)) % GRID)
    second = np.zeros((2, HALF, GROUPS * GRID))
    second[0, : len(disc)] = np.cos(angle)
    second[1, : len(disc)] = np.sin(angle)
    second = second.reshape(2 * HALF, GROUPS * GRID)
    angle = theta * ((ky[:, None] * np.repeat(np.arange(4), 2 * KZ)[None, :]) % GRID)
    turn = np.tile(np.repeat([1.0, -1.0], KZ), 4)
    twiddle = np.zeros((2, HALF, 8 * KZ), np.float32)
    twiddle[0, : len(disc)] = np.cos(angle)
    twiddle[1, : len(disc)] = np.sin(angle) * turn
    column = np.full((2, HALF), -1, np.int32)
    column[0, : len(disc)] = (kx % KB) * KB + ky % KB
    column[1, 1 : len(disc)] = ((-kx) % KB)[1:] * KB + ((-ky) % KB)[1:]
    first_hi, first_lo = split(first)
    first = np.concatenate([first_hi, first_lo], axis=1)
    second = np.concatenate(split(second), axis=0)
    return first, second, twiddle, column.reshape(2 * HALF, 1)


MESH = pl.DeviceIdType.MESH
KINDS = 9


def gather_steps(send, recv, shard, piece, hi, ring, device_of, landed=lambda i: None, ring_first=False):
    own = hi * 4 + ring
    mate = (1 - hi) * 4 + ring
    right, left, far = lax.rem(ring + 1, 4), lax.rem(ring + 3, 4), lax.rem(ring + 2, 4)

    def copy(kind, ref, target):
        return pltpu.make_async_remote_copy(
            src_ref=ref,
            dst_ref=ref,
            send_sem=send.at[kind],
            recv_sem=recv.at[kind],
            device_id=device_of(target),
            device_id_type=MESH,
        )

    to_right, to_left = hi * 4 + right, hi * 4 + left
    from_left, from_right, across = hi * 4 + left, hi * 4 + right, hi * 4 + far
    mate_left, mate_right, mate_across = (1 - hi) * 4 + left, (1 - hi) * 4 + right, (1 - hi) * 4 + far

    if ring_first:
        relays = [(3, shard(from_left), mate), (4, shard(from_right), mate)]
        relays += [(5, piece(from_left, 0), to_right), (6, piece(from_right, 1), to_left)]
        relays += [(7, piece(across, 0), mate), (8, piece(across, 1), mate)]
    else:
        relays = [(3, shard(mate), to_right), (4, shard(mate), to_left)]
        relays += [(5, piece(from_left, 0), to_right), (6, piece(from_right, 1), to_left)]
        relays += [(7, piece(mate_left, 0), to_right), (8, piece(mate_right, 1), to_left)]
    sends = [
        (0, shard(own), mate),
        (1, shard(own), to_right),
        (2, shard(own), to_left),
    ] + relays
    landings = [
        shard(mate),
        shard(from_left),
        shard(from_right),
        shard(mate_left),
        shard(mate_right),
        piece(across, 0),
        piece(across, 1),
        piece(mate_across, 0),
        piece(mate_across, 1),
    ]

    def start(*kinds):
        for kind in kinds:
            copy(*sends[kind]).start()

    def arrived(*kinds):
        for kind in kinds:
            copy(kind, landings[kind], own).wait_recv()

    def begin():
        start(0, 1, 2)
        landed(own)

    def mid():
        if ring_first:
            arrived(1)
            start(5, 3)
            arrived(2)
            start(6, 4)
        else:
            arrived(0)
            start(3, 4)
            arrived(1)
            start(5)
            arrived(2)
            start(6)
        landed(mate)
        landed(from_left)
        landed(from_right)

    def late():
        if ring_first:
            arrived(5)
            start(7)
            arrived(6)
            start(8)
            return
        arrived(3)
        start(7)
        arrived(4)
        start(8)
        landed(mate_left)
        landed(mate_right)

    def finish():
        if ring_first:
            arrived(0, 3, 4, 7, 8)
            return
        arrived(5, 6, 7, 8)
        landed(across)
        landed(mate_across)

    def sent():
        for kind in range(KINDS):
            copy(*sends[kind]).wait_send()

    return begin, mid, late, finish, sent


def pair_kernel(
    weight, occ_in, emp_in, first, second, tw, out,
    occ, emp, z_hi, z_lo, high_0, low_0, high_1, low_1, local, o_send, o_recv, e_send, e_recv, s_send, s_recv,
):
    n_occ, n_emp = occ.shape[0], emp.shape[0]
    o = lax.axis_index("occ")
    m = lax.axis_index("emp")
    o_hi, o_ring = o // 4, lax.rem(o, 4)
    chip, core = m // 2, lax.rem(m, 2)
    c_hi, c_ring = chip // 4, lax.rem(chip, 4)

    def emp_band(c):
        return gather_steps(
            e_send.at[c], e_recv.at[c],
            lambda i: emp.at[c, :, i],
            lambda i, h: emp.at[c, h, i],
            o_hi, o_ring,
            lambda i: {"occ": i, "emp": m},
            ring_first=c in RING_FIRST,
        )

    def occ_band(v):
        return gather_steps(
            o_send.at[v], o_recv.at[v],
            lambda i: occ.at[v, core, i],
            lambda i, h: occ.at[v, core, i, h],
            c_hi, c_ring,
            lambda i: {"occ": o, "emp": 2 * i + core},
        )

    sibling = {"occ": o, "emp": 2 * chip + 1 - core}

    def share(v, mine):
        return pltpu.make_async_remote_copy(
            src_ref=occ.at[v, mine],
            dst_ref=occ.at[v, mine],
            send_sem=s_send.at[v],
            recv_sem=s_recv.at[v],
            device_id=sibling,
            device_id_type=MESH,
        )

    copies = []
    for v in range(n_occ):
        copies.append(pltpu.make_async_copy(occ_in.at[v], occ.at[v, core, chip], local.at[v]))
    for c in range(n_emp):
        copies.append(pltpu.make_async_copy(emp_in.at[c], emp.at[c, :, o], local.at[n_occ + c]))
    for copy in copies:
        copy.start()

    barrier = pltpu.get_barrier_semaphore()
    peers = [
        {"occ": (1 - o_hi) * 4 + o_ring, "emp": m},
        {"occ": o_hi * 4 + lax.rem(o_ring + 1, 4), "emp": m},
        {"occ": o_hi * 4 + lax.rem(o_ring + 3, 4), "emp": m},
        {"occ": o, "emp": 2 * ((1 - c_hi) * 4 + c_ring) + core},
        {"occ": o, "emp": 2 * (c_hi * 4 + lax.rem(c_ring + 1, 4)) + core},
        {"occ": o, "emp": 2 * (c_hi * 4 + lax.rem(c_ring + 3, 4)) + core},
        sibling,
    ]
    for peer in peers:
        pl.semaphore_signal(barrier, inc=1, device_id=peer, device_id_type=MESH)
    pl.semaphore_wait(barrier, len(peers))
    for copy in copies:
        copy.wait()

    E = [emp_band(c) for c in range(n_emp)]
    O = [occ_band(v) for v in range(n_occ)]

    def pass_on(v):
        O[v][FINISH]()
        share(v, core).start()

    def shared(v):
        share(v, 1 - core).wait_recv()

    for action in (
        E[0][BEGIN],
        O[0][BEGIN],
        O[1][BEGIN],
        O[0][MID],
        E[0][MID],
        O[0][LATE],
        O[2][BEGIN],
        lambda: pass_on(0),
        E[0][LATE],
        E[1][BEGIN],
        O[1][MID],
        O[1][LATE],
        O[3][BEGIN],
        E[0][FINISH],
        lambda: shared(0),
    ):
        action()

    steps = {
        2: (lambda: pass_on(1),),
        3: (E[1][MID], E[2][BEGIN],),
        4: (lambda: shared(1), O[2][MID],),
        6: (E[1][LATE],),
        7: (O[2][LATE],),
        8: (lambda: pass_on(2), lambda: shared(2),),
        10: (O[3][MID],),
        12: (E[1][FINISH], E[2][MID], E[3][BEGIN],),
        13: (O[3][LATE],),
        15: (lambda: pass_on(3),),
        17: (E[2][LATE],),
        18: (lambda: shared(3),),
        21: (E[3][MID],),
        25: (E[3][LATE],),
        32: (E[2][FINISH],),
        48: (E[3][FINISH],),
    }

    pairs = n_occ * n_emp
    highs, lows = (high_0, high_1), (low_0, low_1)

    def pair_at(n):
        late, extra = n // 8, n // 6
        early = 1 - late
        first_six = early * (1 - lax.rem(extra, 2))
        pair_of_last = early - first_six
        c = first_six * (n // 3) + pair_of_last * (n - 6) + late * (n // 4)
        v = first_six * lax.rem(n, 3) + pair_of_last * 3 + late * lax.rem(n, 4)
        return v, c

    def products(n, t):
        v, c = pair_at(n)
        high_to, low_to = highs[t % 2], lows[t % 2]
        for i in range(TILE):
            slab = t * TILE + i
            h, s = slab // 8, slab % 8
            rows = slice(i * ROWS, (i + 1) * ROWS)
            for q in range(3):
                vr = occ[v, h, s, 0, q].astype(f32)
                vi = occ[v, h, s, 1, q].astype(f32)
                cr = emp[c, h, s, 0, q].astype(f32)
                ci = emp[c, h, s, 1, q].astype(f32)
                for at, p in ((0, vr * cr + vi * ci), (1, vr * ci - vi * cr)):
                    lanes = slice((2 * q + at) * 128, (2 * q + at + 1) * 128)
                    high = p.astype(bf16)
                    high_to[rows, lanes] = high
                    low_to[rows, lanes] = (p - high.astype(f32)).astype(bf16)

    def transform_z(t):
        high, low = highs[t % 2], lows[t % 2]
        parts = []
        for q in range(3):
            table = first[q * 256 : (q + 1) * 256, :]
            chunk = slice(q * 256, (q + 1) * 256)
            both = jnp.dot(high[:, chunk], table, preferred_element_type=f32)
            more = jnp.dot(low[:, chunk], table[:, :128], preferred_element_type=f32)
            parts.append(both[:, :128] + (both[:, 128:] + more))
        upper = lax.broadcasted_iota(jnp.int32, parts[1].shape, 1) >= 64
        zero = jnp.zeros_like(parts[1])
        for at, z in (
            (0, parts[0] + jnp.where(upper, parts[1], zero)),
            (1, parts[2] + jnp.where(upper, zero, parts[1])),
        ):
            where = (slice(t * TILE * ROWS, (t + 1) * TILE * ROWS), slice(at * 128, (at + 1) * 128))
            high_z = z.astype(bf16)
            z_hi[where] = high_z
            z_lo[where] = (z - high_z.astype(f32)).astype(bf16)

    def swap(a):
        real = lax.rem(lax.broadcasted_iota(jnp.int32, a.shape, 1) // KZ, 2) == 0
        return jnp.where(real, pltpu.roll(a, a.shape[1] - KZ, 1), pltpu.roll(a, KZ, 1))

    def transform_xy(n):
        v, c = pair_at(n)
        big = jnp.dot(second[...], z_hi[...], preferred_element_type=f32)
        small = jnp.dot(second[: 2 * HALF, :], z_lo[...], preferred_element_type=f32)
        both = big[: 2 * HALF] + (big[2 * HALF :] + small)
        u = both[:HALF]
        real = lax.rem(lax.broadcasted_iota(jnp.int32, u.shape, 1) // KZ, 2) == 0
        w = swap(both[HALF:])
        w = jnp.where(real, w, -w)
        cos, sin = tw[0], tw[1]
        scale = weight[v, c]
        for sign in range(2):
            g = u + w if sign == 0 else u - w
            turned = sin * swap(g)
            full = (cos * g + turned if sign == 0 else cos * g - turned).T
            total = (full[: 2 * KZ] + full[2 * KZ : 4 * KZ]) + (full[4 * KZ : 6 * KZ] + full[6 * KZ :])
            total = (total * scale).astype(bf16).reshape(2, KZ, HALF)
            out[:, v, c, :, sign * HALF : (sign + 1) * HALF] = total

    products(0, 0)

    tiles = 16 // TILE

    def serve(n, t):
        for step, actions in steps.items():
            if step % tiles == t:

                @pl.when(n == step // tiles)
                def _(actions=actions):
                    for action in actions:
                        action()

    def one_pair(n, carry):
        for t in range(tiles):
            transform_z(t)
            if t + 1 < tiles:
                serve(n, t + 1)
                products(n, t + 1)
        serve(n + 1, 0)
        transform_xy(n)
        products(jnp.minimum(n + 1, pairs - 1), 0)
        return carry

    lax.fori_loop(0, pairs, one_pair, 0)
    for v in range(n_occ):
        O[v][SENT]()
        share(v, core).wait_send()
    for c in range(n_emp):
        E[c][SENT]()


TILE = 4


def compact(weight, occupied, empty):
    first, second, tw, unused = tables()
    n_occ, n_emp = occupied.shape[1], empty.shape[1]
    occ_in = occupied.reshape(2, n_occ, SLAB, GROUPS, 3, 128).transpose(1, 0, 4, 3, 2, 5)
    occ_in = occ_in.reshape(n_occ, 2, 3, ROWS, 128)
    emp_in = empty.reshape(2, n_emp, 2, SLAB, GROUPS, 3, 128).transpose(1, 2, 0, 5, 4, 3, 6)
    emp_in = emp_in.reshape(n_emp, 2, 2, 3, ROWS, 128)
    vmem = pl.BlockSpec(memory_space=pltpu.VMEM)
    hbm = pl.BlockSpec(memory_space=pl.ANY)
    dma = pltpu.SemaphoreType.DMA
    return pl.pallas_call(
        pair_kernel,
        out_shape=jax.ShapeDtypeStruct((2, n_occ, n_emp, KZ, 2 * HALF), bf16),
        in_specs=[pl.BlockSpec(memory_space=pltpu.SMEM), hbm, hbm] + [vmem] * 3,
        out_specs=vmem,
        scratch_shapes=[
            pltpu.VMEM((n_occ, 2, 8, 2, 3, ROWS, 128), bf16),
            pltpu.VMEM((n_emp, 2, 8, 2, 3, ROWS, 128), bf16),
            pltpu.VMEM((GROUPS * GRID, 256), bf16),
            pltpu.VMEM((GROUPS * GRID, 256), bf16),
            pltpu.VMEM((TILE * ROWS, 768), bf16),
            pltpu.VMEM((TILE * ROWS, 768), bf16),
            pltpu.VMEM((TILE * ROWS, 768), bf16),
            pltpu.VMEM((TILE * ROWS, 768), bf16),
            dma((n_occ + n_emp,)),
            dma((n_occ, KINDS)),
            dma((n_occ, KINDS)),
            dma((n_emp, KINDS)),
            dma((n_emp, KINDS)),
            dma((n_occ,)),
            dma((n_occ,)),
        ],
        compiler_params=pltpu.CompilerParams(
            vmem_limit_bytes=60 * 2**20, collective_id=0, has_side_effects=True
        ),
        name="pair_spectra",
    )(weight, occ_in, emp_in, first, second, tw)


def select_kernel(column, kxy, kz, x, out):
    hot = jnp.where(column[...] == kxy[0], 1.0, 0.0).astype(bf16)
    rows = x.shape[0] // KZ
    picked = jnp.dot(x[...], hot, preferred_element_type=f32)
    level = lax.broadcasted_iota(jnp.int32, (KZ, BLOCK_PAD), 0)
    mask = jnp.where(level == kz[0], 1.0, 0.0)
    total = jnp.sum(picked.reshape(rows, KZ, BLOCK_PAD) * mask[None], axis=1)
    out[0] = total.astype(bf16)


def select(gvec, x):
    column = tables()[3]
    blocks = NG // BLOCK
    padded = jnp.pad(gvec.reshape(blocks, 1, BLOCK), ((0, 0), (0, 0), (0, BLOCK_PAD - BLOCK)), constant_values=0)
    kxy = padded // KB
    kz = padded - kxy * KB
    live = lax.broadcasted_iota(jnp.int32, padded.shape, 2) < BLOCK
    kxy = jnp.where(live, kxy, -2)
    rows = x.shape[0] // KZ
    return pl.pallas_call(
        select_kernel,
        grid=(blocks,),
        out_shape=jax.ShapeDtypeStruct((blocks, rows, BLOCK_PAD), bf16),
        in_specs=[
            pl.BlockSpec((2 * HALF, 1), lambda b: (0, 0)),
            pl.BlockSpec((1, 1, BLOCK_PAD), lambda b: (b, 0, 0)),
            pl.BlockSpec((1, 1, BLOCK_PAD), lambda b: (b, 0, 0)),
            pl.BlockSpec(x.shape, lambda b: (0, 0)),
        ],
        out_specs=pl.BlockSpec((1, rows, BLOCK_PAD), lambda b: (b, 0, 0)),
        compiler_params=pltpu.CompilerParams(vmem_limit_bytes=40 * 2**20),
        name="sphere_select",
    )(column, kxy, kz, x)


def densities_of(occ_all, emp_all, occ_energy, emp_energy, gvec):
    weight = jnp.sqrt(4.0 / (emp_energy[None, :] - occ_energy[:, None])) / math.sqrt(GRID**3)
    x = compact(weight, occ_all, emp_all)
    rows = 2 * x.shape[1] * x.shape[2]
    return select(gvec, x.reshape(rows * KZ, 2 * HALF))


BEGIN, MID, LATE, FINISH, SENT = range(5)


def chi_kernel(factor, d, out, rows, cols, local, r_send, r_recv, c_send, c_recv, g_send, g_recv, s_send, s_recv):
    o = lax.axis_index("occ")
    m = lax.axis_index("emp")
    o_hi, o_ring = o // 4, lax.rem(o, 4)
    chip, core = m // 2, lax.rem(m, 2)
    c_hi, c_ring = chip // 4, lax.rem(chip, 4)

    def copy(src, dst, send, recv, device):
        return pltpu.make_async_remote_copy(
            src_ref=src, dst_ref=dst, send_sem=send, recv_sem=recv, device_id=device, device_id_type=MESH
        )

    own_copies = [pltpu.make_async_copy(d.at[2 * o + b], rows.at[b, core, o, chip], local.at[b]) for b in range(2)]
    own_copies.append(pltpu.make_async_copy(d.at[m], cols.at[core, o, chip], local.at[2]))
    for own_copy in own_copies:
        own_copy.start()

    barrier = pltpu.get_barrier_semaphore()
    for step in range(1, 8):
        peer = {"occ": lax.rem(o + step, 8), "emp": m}
        pl.semaphore_signal(barrier, inc=1, device_id=peer, device_id_type=MESH)
    for step in range(1, 16):
        peer = {"occ": o, "emp": lax.rem(m + step, 16)}
        pl.semaphore_signal(barrier, inc=1, device_id=peer, device_id_type=MESH)
    pl.semaphore_wait(barrier, 22)

    def row_part(b, step):
        to = lax.rem(o + step, 8)
        return copy(
            d.at[2 * to + b], rows.at[b, core, o, chip], r_send.at[b, step - 1], r_recv.at[b, step - 1],
            {"occ": to, "emp": m},
        )

    def row_landing(b, step):
        here = rows.at[b, core, lax.rem(o + 8 - step, 8), chip]
        return copy(here, here, r_send.at[b, step - 1], r_recv.at[b, step - 1], {"occ": o, "emp": m})

    def col_part(step):
        to = lax.rem(m + step, 16)
        return copy(
            d.at[to], cols.at[core, o, chip], c_send.at[step - 1], c_recv.at[step - 1], {"occ": o, "emp": to}
        )

    def col_landing(step):
        source = lax.rem(m + 16 - step, 16)
        here = cols.at[lax.rem(source, 2), o, source // 2]
        return copy(here, here, c_send.at[step - 1], c_recv.at[step - 1], {"occ": o, "emp": m})

    row_steps = range(1, 8)
    even, odd = range(2, 16, 2), range(1, 16, 2)
    for step in row_steps:
        row_part(0, step).start()
    for step in even:
        col_part(step).start()
    for step in row_steps:
        row_part(1, step).start()
    for step in odd:
        col_part(step).start()

    sibling = {"occ": o, "emp": 2 * chip + 1 - core}

    def share(b, mine, i):
        here = rows.at[b, mine, :, i]
        return copy(here, here, s_send.at[b, i], s_recv.at[b, i], sibling)

    def row_band(b):
        return gather_steps(
            g_send.at[b], g_recv.at[b],
            lambda i: rows.at[b, core, :, i],
            lambda i, h: rows.at[b, core, pl.ds(4 * h, 4), i],
            c_hi, c_ring,
            lambda i: {"occ": o, "emp": 2 * i + core},
            lambda i: share(b, core, i).start(),
        )

    def col_band(j):
        k = core if j == 0 else 1 - core
        return gather_steps(
            g_send.at[2 + j], g_recv.at[2 + j],
            lambda i: cols.at[k, i],
            lambda i, h: cols.at[k, i, pl.ds(4 * h, 4)],
            o_hi, o_ring,
            lambda i: {"occ": i, "emp": m},
        )

    R = [row_band(b) for b in range(2)]
    C = [col_band(j) for j in range(2)]
    for own_copy in own_copies:
        own_copy.wait()
    for step in row_steps:
        row_landing(0, step).wait_recv()
    R[0][BEGIN]()
    for step in even:
        col_landing(step).wait_recv()
    C[0][BEGIN]()
    for step in row_steps:
        row_landing(1, step).wait_recv()
    R[1][BEGIN]()
    for step in odd:
        col_landing(step).wait_recv()
    C[1][BEGIN]()
    for part in (MID, LATE):
        for band in (R[0], C[0], R[1], C[1]):
            band[part]()
    R[0][FINISH]()
    C[0][FINISH]()
    R[1][FINISH]()

    depth = rows.shape[2] * rows.shape[3] * rows.shape[4]
    half = rows.shape[4] // 2

    def multiply(k, blocks, last):
        right = cols[k].reshape(depth // (2 * half), 2 * half, BLOCK_PAD)
        turned = jnp.concatenate([-right[:, half:], right[:, :half]], axis=1)
        right = right.reshape(depth, BLOCK_PAD)
        turned = turned.reshape(depth, BLOCK_PAD)
        for b in blocks:
            left = rows[b, k].reshape(depth, BLOCK_PAD)
            for at, side in ((0, right), (1, turned)):
                part = lax.dot_general(left, side, (((0,), (0,)), ((), ())), preferred_element_type=f32)
                part = part[:BLOCK, :BLOCK]
                out[at, b] = (out[at, b] + part) * factor if last else part

    multiply(core, (0, 1), False)
    C[1][FINISH]()
    for b in range(2):
        for i in range(8):
            share(b, 1 - core, i).wait_recv()
    multiply(1 - core, (0, 1), True)
    for step in row_steps:
        for b in range(2):
            row_part(b, step).wait_send()
    for step in range(1, 16):
        col_part(step).wait_send()
    for band in R + C:
        band[SENT]()
    for b in range(2):
        for i in range(8):
            share(b, core, i).wait_send()


def body(occupied, empty, occ_energy, emp_energy, gvec):
    d = densities_of(occupied, empty, occ_energy, emp_energy, gvec)
    rows = d.shape[1]
    n_occ = lax.axis_size("occ")
    n_emp = lax.axis_size("emp")
    factor = -1.0 / math.sqrt(n_occ * n_emp * (rows // 2))
    vmem = pl.BlockSpec(memory_space=pltpu.VMEM)
    dma = pltpu.SemaphoreType.DMA
    chi = pl.pallas_call(
        functools.partial(chi_kernel, factor),
        out_shape=jax.ShapeDtypeStruct((2, 2, BLOCK, BLOCK), f32),
        in_specs=[pl.BlockSpec(memory_space=pl.ANY)],
        out_specs=vmem,
        scratch_shapes=[
            pltpu.VMEM((2, 2, 8, 8, rows, BLOCK_PAD), bf16),
            pltpu.VMEM((2, 8, 8, rows, BLOCK_PAD), bf16),
            dma((3,)),
            dma((2, 7)),
            dma((2, 7)),
            dma((15,)),
            dma((15,)),
            dma((4, KINDS)),
            dma((4, KINDS)),
            dma((2, 8)),
            dma((2, 8)),
        ],
        compiler_params=pltpu.CompilerParams(
            vmem_limit_bytes=56 * 2**20, collective_id=1, has_side_effects=True
        ),
        name="chi_blocks",
    )(d)
    return chi.reshape(2, 2 * BLOCK, BLOCK)


def solution(mesh):
    placed = (P(None, "occ", "emp", None), P(None, "emp", "occ", None), P("occ"), P("emp"), P())
    return jax.shard_map(
        body, mesh=mesh, in_specs=placed, out_specs=P(None, "occ", "emp"), check_vma=False
    )
```
